256 devices in a mesh: batch: 8 (over y, z_lo), latent: 32 (over z_hi, x, core).
Axes of the slice: x: 4, y: 4, z: 8 (z_hi: 4, z_lo: 2; z = z_hi * 2 + z_lo), core: 2. Of those that a mesh axis runs over, the one named last changes fastest.
Arguments:
- activations: bfloat16 [512, 3584], P(('batch', 'latent')), may hold values from -16 to 16
- indices: int32 [512, 64], P(('batch', 'latent')), may hold values from 0 to 98303, as said below
- enc_weight: bfloat16 [3584, 98304], P(None, ('batch', 'latent')), may hold values from -0.09375 to 0.09375
- dec_weight: bfloat16 [98304, 3584], P(('batch', 'latent')), may hold values from -0.75 to 0.75
- enc_bias: bfloat16 [98304], P(('batch', 'latent')), may hold values from -3 to 3
- dec_bias: float32 [3584], replicated, may hold values from -3 to 3
Outputs:
- mse_loss: float32 [], replicated
- grad_enc: bfloat16 [3584, 98304], P(None, ('batch', 'latent'))
- grad_dec: bfloat16 [98304, 3584], P(('batch', 'latent'))
- grad_encbias: float32 [98304], P(('batch', 'latent'))
- grad_decbias: float32 [3584], replicated
The draws below stay inside these ranges and needn't reach their ends.
Inputs may be any that keep to these rules, and one draw needn't show every extreme that they name: `indices`: the 64 active latents of a row are distinct; exactly 8 of them lie on the devices of each batch index; and among the 16 rows held by the devices of one latent index, exactly 4 active latents lie on each device whose batch index is a given one.
All inputs are finite; a program needn't handle non-finite values.
Results may differ from the reference program's by a relative error of at most 0.015.
Values may be sent and summed in bfloat16 or wider, within the bound.
No kernel may reach another device: no remote copies, remote signals or barrier semaphores. Data moves between devices by JAX's collectives and lax.ppermute only.
A program may use at most 128 MiB of HBM per device.

```python
import jax
import jax.numpy as jnp
from jax import lax

D = 3584
K = 64
LAT_DEV = 384
ROW_DEV = 2
ROWS = 512
LATENTS = 98304
N_BATCH = 8
N_LATENT = 32


def draw_activations(key, part):
    key = jax.random.fold_in(key, 11)
    k_row, k_col, k_base = jax.random.split(key, 3)
    ramp = 1.0 + 2.0 * jnp.arange(ROWS, dtype=jnp.float32)[:, None] / (ROWS - 1)
    row_scale = jnp.exp(jax.random.uniform(k_row, (ROWS, 1), jnp.float32, -1.15, 1.15))
    col_scale = jnp.exp(jax.random.uniform(k_col, (1, D), jnp.float32, -0.8, 0.8))
    base = jax.random.normal(k_base, (ROWS, D), jnp.float32)
    return jnp.clip(0.4 * base * ramp * row_scale * col_scale, -16.0, 16.0).astype(jnp.bfloat16)


def draw_indices(key, part):
    key = jax.random.fold_in(key, 23)
    k_perm, k_local, k_order = jax.random.split(key, 3)
    group_k = K // N_BATCH
    perm_keys = jax.random.split(k_perm, N_LATENT * N_BATCH)
    owner_perm = jax.vmap(lambda single: jax.random.permutation(single, N_LATENT))(perm_keys).reshape(N_LATENT, N_BATCH, N_LATENT).astype(jnp.int32)
    row_index = jnp.arange(ROWS, dtype=jnp.int32)
    device = row_index // ROW_DEV
    lat_pos = device % N_LATENT
    batch_pos = device // N_LATENT
    within = batch_pos * ROW_DEV + row_index % ROW_DEV
    slot = jnp.arange(group_k, dtype=jnp.int32)
    place = (within[:, None, None] * group_k + slot[None, None, :]) % N_LATENT
    owner_batch = jnp.arange(N_BATCH, dtype=jnp.int32)[None, :, None]
    owner_lat = owner_perm[lat_pos[:, None, None], owner_batch, place]
    offsets = jax.random.randint(k_local, (ROWS, N_BATCH, N_LATENT), 0, LAT_DEV, dtype=jnp.int32)
    pick = jnp.broadcast_to(slot % N_LATENT, (ROWS, N_BATCH, group_k))
    local = (jnp.take_along_axis(offsets, pick, axis=2) + slot[None, None, :] // N_LATENT) % LAT_DEV
    latent = (owner_batch * N_LATENT + owner_lat) * LAT_DEV + local
    flat = latent.reshape(ROWS, K).astype(jnp.int32)
    order_keys = jax.random.split(k_order, ROWS)
    shuffle = jax.vmap(lambda single: jax.random.permutation(single, K))(order_keys).astype(jnp.int32)
    return jnp.take_along_axis(flat, shuffle, axis=1).astype(jnp.int32)


def block_levels(own_key, dims, cuts, smallest, high):
    def one(axis_at, blocks):
        draws = jax.random.uniform(jax.random.fold_in(jax.random.fold_in(own_key, 6), axis_at), (blocks,), jnp.float32, smallest / len(cuts), high / len(cuts))
        return jnp.repeat(jnp.exp(draws), dims[axis_at] // blocks).reshape((-1,) + (1,) * (len(dims) - axis_at - 1))

    level = one(*cuts[0])
    for cut in cuts[1:]:
        level = level * one(*cut)
    return level


def normal_values(key, shape, scale, most, cuts=(), kind=jnp.bfloat16):
    result = jax.random.normal(key, shape, jnp.float32) * scale
    if len(cuts) > 0:
        result = block_levels(key, shape, cuts, -0.22, 0.18) * result
    return jnp.clip(result, min=-most, max=most).astype(kind)


def setup_inputs(seed: int = 0) -> dict:
    seeds = jax.random.split(jax.random.key(seed), 7)
    activations = draw_activations(jax.random.fold_in(seeds[6], 71), 0)
    indices = draw_indices(jax.random.fold_in(seeds[6], 71), 0)
    enc_weight = normal_values(seeds[2], (D, LATENTS), D ** -0.5, 0.09375, ((1, 256),))
    dec_weight = normal_values(seeds[3], (LATENTS, D), K ** -0.5, 0.75, ((0, 256),))
    enc_bias = normal_values(seeds[4], (LATENTS,), 0.5, 3.0, ((0, 256),))
    dec_bias = normal_values(seeds[5], (D,), 0.5, 3.0, (), jnp.float32)
    return dict(activations=activations, indices=indices, enc_weight=enc_weight, dec_weight=dec_weight, enc_bias=enc_bias, dec_bias=dec_bias)


def reference(activations, indices, enc_weight, dec_weight, enc_bias, dec_bias):
    centred = (activations.astype(jnp.float32) - dec_bias[None, :]).astype(jnp.bfloat16)
    preact = jnp.dot(centred, enc_weight, preferred_element_type=jnp.float32) + enc_bias.astype(jnp.float32)[None, :]
    row_ids = jnp.broadcast_to(jnp.arange(ROWS, dtype=jnp.int32)[:, None], indices.shape)
    selected = jnp.zeros((ROWS, LATENTS), jnp.float32).at[row_ids, indices].set(1.0)
    codes = (selected * preact).astype(jnp.bfloat16)
    rebuilt = jnp.dot(codes, dec_weight, preferred_element_type=jnp.float32)
    residual = rebuilt - centred.astype(jnp.float32)
    mse_loss = jnp.sum(residual * residual) / (ROWS * D)
    grad_out = residual.astype(jnp.bfloat16)
    back_codes = lax.dot_general(grad_out, dec_weight, (((1,), (1,)), ((), ())), preferred_element_type=jnp.float32)
    grad_pre = (selected * back_codes).astype(jnp.bfloat16)
    grad_encbias = jnp.sum(grad_pre.astype(jnp.float32), axis=0)
    blocks = jnp.arange(LATENTS // LAT_DEV, dtype=jnp.int32)

    def per_block(block_index):
        row_start = block_index * LAT_DEV
        code_block = lax.dynamic_slice_in_dim(codes, row_start, LAT_DEV, 1)
        pre_block = lax.dynamic_slice_in_dim(grad_pre, row_start, LAT_DEV, 1)
        dec_block = lax.dynamic_slice_in_dim(dec_weight, row_start, LAT_DEV, 0)
        enc_block = lax.dynamic_slice_in_dim(enc_weight, row_start, LAT_DEV, 1)
        bias_block = lax.dynamic_slice_in_dim(grad_encbias, row_start, LAT_DEV, 0)
        enc_grad = lax.dot_general(centred, pre_block, (((0,), (0,)), ((), ())), preferred_element_type=jnp.float32).astype(jnp.bfloat16)
        raw_dec = lax.dot_general(code_block, grad_out, (((0,), (0,)), ((), ())), preferred_element_type=jnp.float32)
        dec_float = dec_block.astype(jnp.float32)
        along_row = jnp.sum(raw_dec * dec_float, axis=1)
        norm_sq = jnp.sum(dec_float * dec_float, axis=1) + 1e-6
        dec_grad = (raw_dec - (along_row / norm_sq)[:, None] * dec_float).astype(jnp.bfloat16)
        enc_term = jnp.dot(enc_block.astype(jnp.float32), bias_block, precision=lax.Precision.HIGHEST)
        return enc_grad, dec_grad, enc_term

    enc_parts, dec_parts, enc_terms = lax.map(per_block, blocks)
    grad_enc = jnp.transpose(enc_parts, (1, 0, 2)).reshape(D, LATENTS)
    grad_dec = dec_parts.reshape(LATENTS, D)
    grad_decbias = jnp.sum(residual, axis=0) - jnp.sum(enc_terms, axis=0)
    return (mse_loss, grad_enc, grad_dec, grad_encbias, grad_decbias)
```

```python
import functools

import jax
import jax.numpy as jnp
from jax import lax
from jax.experimental import pallas as pl
from jax.experimental.pallas import tpu as pltpu
from jax.sharding import PartitionSpec as P

bf16 = jnp.bfloat16
f32 = jnp.float32

D = 3584
HALF = D // 2
QUARTER = D // 4
LAT = 384
NB = 8
NL = 32
SLOTS = 4
K = 64
PAIR_ROWS = NL * 2 * SLOTS
HOME_ROWS = NB * 2 * 4
ROWS = 512
IDS = 128
VEC = D + 128


def dot(a, b, dims=((1,), (0,))):
    return lax.dot_general(a, b, (dims, ((), ())), preferred_element_type=f32)


def iota(shape, axis):
    return lax.broadcasted_iota(jnp.int32, shape, axis)


def dispatch(onehot, rows, out_ref):
    for j in range(2):
        pick = onehot[:, j * HOME_ROWS : (j + 1) * HOME_ROWS]
        out_ref[:, j * QUARTER : (j + 1) * QUARTER] = dot(pick, rows).astype(bf16)


def route_kernel(batch_ref, home_ref, out_ref, onehot_ref):
    me = batch_ref[0]
    row = iota((PAIR_ROWS, IDS), 0)
    lane = iota((PAIR_ROWS, IDS), 1)
    device = (me * NL + row // (2 * SLOTS)).astype(f32)
    slot = (row % SLOTS + 1).astype(f32)
    half = (row // SLOTS) % 2
    upper = (iota((IDS, IDS), 0) <= iota((IDS, IDS), 1)).astype(bf16)
    entry = iota((IDS, IDS), 0)
    column = iota((IDS, IDS), 1)
    before = jnp.zeros((PAIR_ROWS, 1), f32)
    pick = jnp.zeros((PAIR_ROWS, IDS), f32)
    ids = jnp.zeros((PAIR_ROWS, IDS), f32)
    for b in range(NB):
        block = home_ref[b * 8 : (b + 1) * 8, QUARTER:]
        ours = block[0:1, :].astype(f32) == device
        count = dot(ours.astype(bf16), upper)
        chosen = (ours & (count + before == slot)).astype(bf16)
        before = before + count[:, IDS - 1 :]
        owner_row = 2 * b + entry // K
        pick = pick + dot(chosen, (owner_row == (column % HOME_ROWS) // 4).astype(bf16))
        padded = jnp.concatenate([block, jnp.zeros((IDS - 8, IDS), bf16)], axis=0)
        ids = ids + dot(chosen, padded, ((1,), (1,)))
    quarter = column[0:1, :] % 4
    wanted = 2 * half + lane // HOME_ROWS
    onehot = jnp.where(quarter == wanted, pick, 0.0).astype(bf16)
    onehot_ref[...] = onehot
    dispatch(onehot, home_ref[:, :QUARTER], out_ref)
    out_ref[:, HALF:] = ids.astype(bf16)


def both_halves(t):
    t = t.reshape(NL, 2 * SLOTS, LAT)
    return (t + pltpu.roll(t, SLOTS, 1)).reshape(PAIR_ROWS, LAT)


def first_half():
    return (iota((PAIR_ROWS, 1), 0) // SLOTS) % 2 == 0


def code_kernel(x_ref, enc_ref, dec_ref, bias_ref, y_ref, code_ref, sel_ref):
    hi = x_ref[:, HALF + 1 : HALF + 2].astype(f32)
    lo = x_ref[:, HALF + 2 : HALF + 3].astype(f32)
    sel = (hi * 128.0 + lo == iota((PAIR_ROWS, LAT), 1).astype(f32)).astype(f32)
    sel_ref[...] = sel.astype(bf16)
    x = x_ref[:, :HALF]
    first = first_half()
    t = jnp.where(first, dot(x, enc_ref[:HALF, :]), dot(x, enc_ref[HALF:, :]))
    codes = (sel * (both_halves(t) + bias_ref[...].astype(f32))).astype(bf16)
    code_ref[...] = codes
    y_ref[...] = jnp.where(
        first, dot(codes, dec_ref[:, :HALF]), dot(codes, dec_ref[:, HALF:])
    ).astype(bf16)


def collect_kernel(y_ref, onehot_ref, out_ref):
    total = jnp.zeros((HOME_ROWS, QUARTER), f32)
    for j in range(2):
        pick = onehot_ref[:, j * HOME_ROWS : (j + 1) * HOME_ROWS]
        total = total + dot(pick, y_ref[:, j * QUARTER : (j + 1) * QUARTER], ((0,), (0,)))
    total = total.astype(bf16)
    for b in range(NB):
        out_ref[b * HOME_ROWS : (b + 1) * HOME_ROWS, :] = total


def residual_kernel(parts_ref, home_ref, onehot_ref, out_ref, sums_ref):
    rebuilt = parts_ref[:HOME_ROWS, :].astype(f32)
    for b in range(1, NB):
        rebuilt = rebuilt + parts_ref[b * HOME_ROWS : (b + 1) * HOME_ROWS, :].astype(f32)
    residual = rebuilt - home_ref[:, :QUARTER].astype(f32)
    dispatch(onehot_ref[...], residual.astype(bf16), out_ref)
    columns = jnp.sum(residual.reshape(NB, 8, QUARTER), axis=0) * (1.0 / NB)
    for q in range(4):
        sums_ref[:, q * QUARTER : (q + 1) * QUARTER] = columns[q : q + 1] + columns[q + 4 : q + 5]
    square = jnp.sum(residual * residual) * (1.0 / (NB * ROWS * D))
    sums_ref[:, D:] = jnp.full((1, VEC - D), square, f32)


def pre_kernel(g_ref, enc_ref, dec_ref, sel_ref, sums_ref, pre_ref, bias_ref, vec_ref):
    g = g_ref[...]
    first = first_half()
    t = jnp.where(
        first,
        dot(g, dec_ref[:, :HALF], ((1,), (1,))),
        dot(g, dec_ref[:, HALF:], ((1,), (1,))),
    )
    pre = (sel_ref[...].astype(f32) * both_halves(t)).astype(bf16)
    pre_ref[...] = pre
    bias = jnp.sum(jnp.where(first, pre.astype(f32), 0.0), axis=0, keepdims=True)
    bias_ref[...] = bias
    a = bias.astype(bf16)
    rest = bias - a.astype(f32)
    b = rest.astype(bf16)
    c = (rest - b.astype(f32)).astype(bf16)
    split = jnp.concatenate([a, b, c, jnp.zeros((13, LAT), bf16)], axis=0)
    term = dot(split, enc_ref[...], ((1,), (1,)))
    vec_ref[:, :D] = sums_ref[:, :D] - (term[0:1] + (term[1:2] + term[2:3]))
    vec_ref[:, D:] = sums_ref[:, D:]


def grads_kernel(x_ref, g_ref, pre_ref, code_ref, dec_ref, genc_ref, gdec_ref, raw_ref):
    first = first_half()
    zero = jnp.zeros((), f32)
    pre = pre_ref[...].astype(f32)
    code = code_ref[...].astype(f32)
    along = jnp.zeros((LAT, 1), f32)
    norm = jnp.zeros((LAT, 1), f32)
    for h in range(2):
        mine = first if h == 0 else jnp.logical_not(first)
        part = slice(h * HALF, (h + 1) * HALF)
        pre_h = jnp.where(mine, pre, zero).astype(bf16)
        genc_ref[part, :] = dot(x_ref[:, :HALF], pre_h, ((0,), (0,))).astype(bf16)
        code_h = jnp.where(mine, code, zero).astype(bf16)
        raw = dot(code_h, g_ref[...], ((0,), (0,)))
        raw_ref[:, part] = raw
        dec = dec_ref[:, part].astype(f32)
        along = along + jnp.sum(raw * dec, axis=1, keepdims=True)
        norm = norm + jnp.sum(dec * dec, axis=1, keepdims=True)
    scale = along / (norm + 1e-06)
    for h in range(2):
        part = slice(h * HALF, (h + 1) * HALF)
        gdec_ref[:, part] = (raw_ref[:, part] - scale * dec_ref[:, part].astype(f32)).astype(bf16)


def call(kernel, outs, *args, scratch=(), smem=0):
    specs = [pl.BlockSpec(memory_space=pltpu.SMEM if i < smem else pltpu.VMEM) for i in range(len(args))]
    return pl.pallas_call(
        kernel,
        out_shape=[jax.ShapeDtypeStruct(s, t) for s, t in outs],
        in_specs=specs,
        out_specs=[pl.BlockSpec(memory_space=pltpu.VMEM) for _ in outs],
        scratch_shapes=list(scratch),
        compiler_params=pltpu.CompilerParams(vmem_limit_bytes=48 * 1024 * 1024),
        name=kernel.__name__,
    )(*args)


def exchange(x, axis, peers):
    shape = x.shape
    x = x.reshape(peers, shape[0] // peers, shape[1])
    return lax.all_to_all(x, axis, split_axis=0, concat_axis=0).reshape(shape)


def local(activations, indices, enc_weight, dec_weight, enc_bias, dec_bias):
    batch = lax.axis_index("batch").astype(jnp.int32).reshape(1)
    centred = (activations.astype(f32) - dec_bias[None, :]).astype(bf16)
    flat = indices.reshape(1, 2 * K)
    inside = flat % LAT
    ids = jnp.concatenate([flat // LAT, inside // 128, inside % 128, jnp.zeros((5, 2 * K), jnp.int32)])
    home = jnp.concatenate([centred.reshape(8, QUARTER), ids.astype(bf16)], axis=1)
    home = jnp.broadcast_to(home[None], (NB, 8, QUARTER + IDS)).reshape(HOME_ROWS, QUARTER + IDS)
    home = exchange(home, "batch", NB)

    sent, onehot = call(
        route_kernel,
        [((PAIR_ROWS, HALF + IDS), bf16), ((PAIR_ROWS, IDS), bf16)],
        batch, home, smem=1,
    )
    x = exchange(sent, "latent", NL)
    y, codes, sel = call(
        code_kernel,
        [((PAIR_ROWS, HALF), bf16), ((PAIR_ROWS, LAT), bf16), ((PAIR_ROWS, LAT), bf16)],
        x, enc_weight, dec_weight, enc_bias.reshape(1, LAT),
    )
    y = exchange(y, "latent", NL)
    (parts,) = call(collect_kernel, [((NB * HOME_ROWS, QUARTER), bf16)], y, onehot)
    parts = exchange(parts, "batch", NB)
    sent, sums = call(
        residual_kernel,
        [((PAIR_ROWS, HALF), bf16), ((1, VEC), f32)],
        parts, home, onehot,
    )
    g = exchange(sent, "latent", NL)
    pre, grad_encbias, vec = call(
        pre_kernel,
        [((PAIR_ROWS, LAT), bf16), ((1, LAT), f32), ((1, VEC), f32)],
        g, enc_weight, dec_weight, sel, sums,
    )
    grad_enc, grad_dec = call(
        grads_kernel,
        [((D, LAT), bf16), ((LAT, D), bf16)],
        x, g, pre, codes, dec_weight,
        scratch=[pltpu.VMEM((LAT, D), f32)],
    )
    for axis, peers in (("batch", NB), ("latent", NL)):
        vec = exchange(jnp.broadcast_to(vec, (peers, VEC)), axis, peers)
        vec = jnp.sum(vec, axis=0, keepdims=True)
    return vec[0, D], grad_enc, grad_dec, grad_encbias.reshape(LAT), vec[0, :D]


def solution(mesh):
    both = ("batch", "latent")
    return jax.shard_map(
        local,
        mesh=mesh,
        in_specs=(P(both, None), P(both, None), P(None, both), P(both, None), P(both), P()),
        out_specs=(P(), P(None, both), P(both, None), P(both), P()),
        check_vma=False,
    )
```

```python
import jax
import jax.numpy as jnp
from jax import lax
from jax.experimental import pallas as pl
from jax.experimental.pallas import tpu as pltpu
from jax.sharding import Mesh, PartitionSpec as P

bf16 = jnp.bfloat16
f32 = jnp.float32

AXES = ("y", "z_lo", "z_hi", "x", "core")
SIZES = (4, 2, 4, 4, 2)
BATCH = ("y", "z_lo")

D = 3584
QUARTER = D // 4
LAT = 384
NB = 8
NZ = 4
NX = 4
NCOL = NB * NZ
SLOTS = 4
K = 64
IDS = 128
WIDE = QUARTER + IDS
PAIRS = 128
CHUNK = PAIRS // NX
BLOCK = 8
HOME = NCOL * BLOCK
PART = NZ * BLOCK
ROWS = 512
VROWS, VCOLS = 8, 512


def dot(a, b, dims=((1,), (0,))):
    return lax.dot_general(a, b, (dims, ((), ())), preferred_element_type=f32)


def iota(shape, axis):
    return lax.broadcasted_iota(jnp.int32, shape, axis)


def quarters(row):
    return [row[:, q * QUARTER : (q + 1) * QUARTER] for q in range(4)]


def fetch(pairs, sems):
    copies = [pltpu.make_async_copy(a, b, sems.at[i]) for i, (a, b) in enumerate(pairs)]
    for c in copies:
        c.start()
    return copies


def setup_kernel(act_hbm, bias_hbm, idx_hbm, out_ref, act_ref, bias_ref, idx_ref, sems):
    for c in fetch([(act_hbm, act_ref), (bias_hbm, bias_ref), (idx_hbm, idx_ref)], sems):
        c.wait()
    centred = act_ref[...].astype(f32) - bias_ref[...].reshape(1, D)
    rows = jnp.concatenate(quarters(centred[0:1]) + quarters(centred[1:2]), axis=0)
    idx = jnp.concatenate([idx_ref[0:1, :], idx_ref[1:2, :]], axis=1)
    third = idx >> 7
    device = (third * 21846) >> 16
    ids = [device, third - 3 * device, idx & 127, jnp.zeros((BLOCK - 3, IDS), jnp.int32)]
    ids = jnp.concatenate([i.astype(f32) for i in ids], axis=0)
    block = jnp.concatenate([rows, ids], axis=1)
    block = jnp.concatenate([block, block], axis=0).astype(bf16)
    for i in range(out_ref.shape[0] // (2 * BLOCK)):
        out_ref[i * 2 * BLOCK : (i + 1) * 2 * BLOCK, :] = block


def take_rows(onehot, own, other, q):
    lane = iota((1, 2 * HOME), 1)
    pick = jnp.where(lane % 4 == q, onehot, jnp.zeros((), bf16))
    return (dot(pick[:, :HOME], own) + dot(pick[:, HOME:], other)).astype(bf16)


def route_kernel(place_ref, own_ref, other_ref, *refs):
    outs, onehot_ref = refs[:NX], refs[NX]
    base, x = place_ref[0], place_ref[1]
    row = iota((NX * SLOTS, IDS), 0)
    device = (base + ((x + row // SLOTS) % NX) * 2).astype(f32)
    slot = (row % SLOTS + 1).astype(f32)
    n = NX * SLOTS
    ids = [own_ref[:, QUARTER:].astype(f32), other_ref[:, QUARTER:].astype(f32)]
    ours = []
    for c in range(2):
        for s in range(NCOL):
            ours.append(jnp.where(ids[c][s * BLOCK : s * BLOCK + 1] == device, 1.0, 0.0))
    upper = (iota((IDS, IDS), 0) <= iota((IDS, IDS), 1)).astype(bf16)
    count = dot(jnp.concatenate(ours, axis=0).astype(bf16), upper)
    chosen = [None] * (2 * NCOL)
    hi, lo = [], []
    for c in range(2):
        for z in range(NZ):
            before = jnp.zeros((n, 1), f32)
            hi_sum = jnp.zeros((n, IDS), f32)
            lo_sum = jnp.zeros((n, IDS), f32)
            for b in range(NB):
                s = b * NZ + z
                at = c * NCOL + s
                here = count[at * n : (at + 1) * n]
                mine = jnp.where(here + before == slot, ours[at], 0.0)
                before = before + here[:, IDS - 1 :]
                chosen[at] = mine
                hi_sum = hi_sum + mine * ids[c][s * BLOCK + 1 : s * BLOCK + 2]
                lo_sum = lo_sum + mine * ids[c][s * BLOCK + 2 : s * BLOCK + 3]
            hi.append(hi_sum)
            lo.append(lo_sum)
    lane = iota((IDS, IDS), 1)
    second = (iota((IDS, IDS), 0) // K == (lane % BLOCK) // 4).astype(bf16)
    spread = dot(jnp.concatenate(chosen, axis=0).astype(bf16), second)
    place = iota((n, IDS), 1) // BLOCK
    per = IDS // BLOCK
    groups = []
    for c in range(2):
        for z in range(NZ):
            tiles = [jnp.zeros((n, IDS), f32) for _ in range(2 * HOME // IDS)]
            for b in range(NB):
                at = c * NCOL + b * NZ + z
                part = jnp.where(place == at % per, spread[at * n : (at + 1) * n], 0.0)
                tiles[at // per] = tiles[at // per] + part
            groups.append(jnp.concatenate(tiles, axis=1))
    to, frm = iota((PAIRS, PAIRS), 0), iota((PAIRS, PAIRS), 1)
    source = ((to // SLOTS) % (2 * NZ)) * n + (to // CHUNK) * SLOTS + to % SLOTS
    order = (frm == source).astype(bf16)
    onehot = dot(order, jnp.concatenate(groups, axis=0).astype(bf16)).astype(bf16)
    onehot_ref[...] = onehot
    hi = dot(order, jnp.concatenate(hi, axis=0).astype(bf16))
    lo = dot(order, jnp.concatenate(lo, axis=0).astype(bf16))
    hi = jnp.sum(hi, axis=1, keepdims=True)
    lo = jnp.sum(lo, axis=1, keepdims=True)
    numbers = jnp.where(lane == 0, hi, jnp.where(lane == 1, lo, 0.0)).astype(bf16)
    for q in range(4):
        rows = take_rows(onehot, own_ref[:, :QUARTER], other_ref[:, :QUARTER], q)
        for d in range(NX):
            outs[d][:, q * QUARTER : (q + 1) * QUARTER] = rows[d * CHUNK : (d + 1) * CHUNK]
    for d in range(NX):
        outs[d][:, D:] = numbers[d * CHUNK : (d + 1) * CHUNK]


def gathered(refs):
    return jnp.concatenate([r[:, :D] for r in refs], axis=0)


PARTS = 4
ENC_ROWS = D // PARTS


def enc_pairs(enc_hbm, enc_ref):
    parts = [pl.ds(i * ENC_ROWS, ENC_ROWS) for i in range(PARTS)]
    return [(enc_hbm.at[p], enc_ref.at[p]) for p in parts]


def code_kernel(x0, x1, x2, x3, enc_hbm, dec_hbm, bias_ref, y0, y1, y2, y3, code_ref, sel_ref, enc_ref, dec_ref, sems):
    copies = fetch(enc_pairs(enc_hbm, enc_ref) + [(dec_hbm, dec_ref)], sems)
    xs = (x0, x1, x2, x3)
    ids = jnp.concatenate([r[:, D:] for r in xs], axis=0).astype(f32)
    number = ids[:, 0:1] * 128.0 + ids[:, 1:2]
    sel = (number == iota((PAIRS, LAT), 1).astype(f32)).astype(f32)
    sel_ref[...] = sel.astype(bf16)
    x = gathered(xs)
    t = jnp.zeros((PAIRS, LAT), f32)
    for i in range(PARTS):
        copies[i].wait()
        part = slice(i * ENC_ROWS, (i + 1) * ENC_ROWS)
        t = t + dot(x[:, part], enc_ref[part, :])
    codes = (sel * (t + bias_ref[...].astype(f32))).astype(bf16)
    code_ref[...] = codes
    code = jnp.sum(codes.astype(f32), axis=1, keepdims=True)
    code = jnp.broadcast_to(code, (PAIRS, IDS)).astype(bf16)
    copies[PARTS].wait()
    y = dot(sel.astype(bf16), dec_ref[...]).astype(bf16)
    for d, out in enumerate((y0, y1, y2, y3)):
        out[:, :D] = y[d * CHUNK : (d + 1) * CHUNK]
        out[:, D:] = code[d * CHUNK : (d + 1) * CHUNK]


def collect_kernel(y0, y1, y2, y3, onehot_ref, own_ref, other_ref):
    ys = (y0, y1, y2, y3)
    y = gathered(ys)
    code = jnp.concatenate([r[:, D:] for r in ys], axis=0).astype(f32)[:, :1]
    coded = (onehot_ref[...].astype(f32) * code).astype(bf16)
    lane = iota((1, 2 * HOME), 1)
    total = jnp.zeros((2 * HOME, QUARTER), f32)
    for q in range(4):
        pick = jnp.where(lane % 4 == q, coded, jnp.zeros((), bf16))
        total = total + dot(pick, y[:, q * QUARTER : (q + 1) * QUARTER], ((0,), (0,)))
    total = total.astype(bf16)
    own_ref[...] = total[:HOME]
    other_ref[...] = total[HOME:]


def add_parts_kernel(parts_ref, wide_ref, out_ref):
    total = parts_ref[:PART, :].astype(f32)
    for b in range(1, NB):
        total = total + parts_ref[b * PART : (b + 1) * PART, :].astype(f32)
    wide_ref[...] = total
    out_ref[...] = total.astype(bf16)


def residual_kernel(place_ref, wide_ref, p1, p2, p3, home_ref, out_ref, sums_ref):
    rebuilt = wide_ref[...] + (p1[...].astype(f32) + p2[...].astype(f32) + p3[...].astype(f32))
    first = pl.multiple_of(place_ref[2] * PART, PART)
    residual = rebuilt - home_ref[pl.ds(first, PART), :QUARTER].astype(f32)
    grad = residual.astype(bf16)
    for b in range(NB):
        out_ref[b * PART : (b + 1) * PART, :] = grad
    columns = jnp.sum(residual.reshape(NZ, BLOCK, QUARTER), axis=0) * (1.0 / NZ)
    for q in range(4):
        sums_ref[:, q * QUARTER : (q + 1) * QUARTER] = columns[q : q + 1] + columns[q + 4 : q + 5]
    square = jnp.sum(residual * residual) * (1.0 / (NZ * ROWS * D))
    sums_ref[:, D:] = jnp.full((1, VCOLS), square, f32)


def dispatch_kernel(onehot_ref, own_ref, other_ref, y0, y1, y2, y3, g0, g1, g2, g3, p0, p1, p2, p3):
    onehot = onehot_ref[...]
    own, other = own_ref[...], other_ref[...]
    y = gathered((y0, y1, y2, y3))
    lane = iota((1, 2 * HOME), 1)
    pre = jnp.zeros((PAIRS, 1), f32)
    for q in range(4):
        rows = take_rows(onehot, own, other, q)
        for d, out in enumerate((g0, g1, g2, g3)):
            out[:, q * QUARTER : (q + 1) * QUARTER] = rows[d * CHUNK : (d + 1) * CHUNK]
        part = y[:, q * QUARTER : (q + 1) * QUARTER]
        pre = pre + jnp.sum(rows.astype(f32) * part.astype(f32), axis=1, keepdims=True)
    pre = jnp.broadcast_to(pre, (PAIRS, IDS)).astype(bf16)
    for d, out in enumerate((p0, p1, p2, p3)):
        out[...] = pre[d * CHUNK : (d + 1) * CHUNK]


def pre_kernel(p0, p1, p2, p3, enc_hbm, sel_ref, sums_ref, pre_ref, bias_ref, vec_ref, enc_ref, sems):
    copies = fetch(enc_pairs(enc_hbm, enc_ref), sems)
    pre = jnp.concatenate([r[...] for r in (p0, p1, p2, p3)], axis=0).astype(f32)[:, :1]
    pre = sel_ref[...].astype(f32) * pre
    pre_ref[...] = pre.astype(bf16)
    bias = jnp.sum(pre, axis=0, keepdims=True)
    bias_ref[...] = bias
    a = bias.astype(bf16)
    rest = bias - a.astype(f32)
    b = rest.astype(bf16)
    c = (rest - b.astype(f32)).astype(bf16)
    split = jnp.concatenate([a, b, c, jnp.zeros((13, LAT), bf16)], axis=0)
    terms = []
    for i in range(PARTS):
        copies[i].wait()
        term = dot(split, enc_ref[i * ENC_ROWS : (i + 1) * ENC_ROWS, :], ((1,), (1,)))
        terms.append(term[0:1] + (term[1:2] + term[2:3]))
    vec = sums_ref[:, :D] - jnp.concatenate(terms, axis=1)
    for i in range(VROWS - 1):
        vec_ref[i : i + 1, :] = vec[:, i * VCOLS : (i + 1) * VCOLS]
    vec_ref[VROWS - 1 :, :] = sums_ref[:, D:]


def grads_kernel(x0, x1, x2, x3, g0, g1, g2, g3, pre_hbm, code_hbm, dec_hbm, genc_ref, gdec_ref, *scratch):
    x_ref, g_ref, pre_ref, code_ref, dec_ref, sems = scratch
    pairs = [(code_hbm, code_ref)]
    for d, r in enumerate((g0, g1, g2, g3)):
        pairs.append((r, g_ref.at[pl.ds(d * CHUNK, CHUNK)]))
    pairs.append((dec_hbm, dec_ref))
    pairs.append((pre_hbm, pre_ref))
    for d, r in enumerate((x0, x1, x2, x3)):
        pairs.append((r, x_ref.at[pl.ds(d * CHUNK, CHUNK)]))
    copies = fetch(pairs, sems)
    for c in copies[: NX + 1]:
        c.wait()
    raw = dot(code_ref[...], g_ref[...], ((0,), (0,)))
    copies[NX + 1].wait()
    dec = dec_ref[...].astype(f32)
    along = jnp.sum(raw * dec, axis=1, keepdims=True)
    norm = jnp.sum(dec * dec, axis=1, keepdims=True)
    gdec_ref[...] = (raw - (along / (norm + 1e-06)) * dec).astype(bf16)
    for c in copies[NX + 2 :]:
        c.wait()
    genc_ref[...] = dot(x_ref[:, :D], pre_ref[...], ((0,), (0,))).astype(bf16)


def vector_kernel(copies, parts_ref, out_ref):
    total = parts_ref[:VROWS, :]
    for i in range(1, parts_ref.shape[0] // VROWS):
        total = total + parts_ref[i * VROWS : (i + 1) * VROWS, :]
    for i in range(copies):
        out_ref[i * VROWS : (i + 1) * VROWS, :] = total


def last_vector_kernel(parts_ref, loss_ref, out_ref):
    total = parts_ref[:VROWS, :]
    for i in range(1, parts_ref.shape[0] // VROWS):
        total = total + parts_ref[i * VROWS : (i + 1) * VROWS, :]
    for i in range(VROWS - 1):
        out_ref[pl.ds(i * VCOLS, VCOLS)] = total[i : i + 1, :].reshape(VCOLS)
    loss_ref[...] = total[VROWS - 1 :, :1]


def pair_vector_kernel(copies, own_ref, other_ref, out_ref):
    total = own_ref[...] + other_ref[...]
    for i in range(copies):
        out_ref[i * VROWS : (i + 1) * VROWS, :] = total


SMEM, VMEM, HBM = pltpu.SMEM, pltpu.VMEM, pltpu.HBM


def call(kernel, name, outs, args, spaces=None, scratch=(), mib=8):
    spaces = spaces or [VMEM] * len(args)
    args = [
        pltpu.with_memory_space_constraint(a, HBM) if s is HBM else a for a, s in zip(args, spaces)
    ]
    return pl.pallas_call(
        kernel,
        out_shape=[jax.ShapeDtypeStruct(s, t) for s, t in outs],
        in_specs=[pl.BlockSpec(memory_space=s) for s in spaces],
        out_specs=[pl.BlockSpec(memory_space=VMEM) for _ in outs],
        scratch_shapes=list(scratch),
        compiler_params=pltpu.CompilerParams(vmem_limit_bytes=mib * 1024 * 1024),
        name=name,
    )(*args)


def exchange(x, axes, peers):
    shape = x.shape
    x = x.reshape(peers, shape[0] // peers, shape[1])
    return lax.all_to_all(x, axes, split_axis=0, concat_axis=0).reshape(shape)


def step(x, axis, size, by):
    return lax.ppermute(x, axis, [(i, (i + by) % size) for i in range(size)])


def swap_cores(x):
    return step(x, "core", 2, 1)


def local(activations, indices, enc_weight, dec_weight, enc_bias, dec_bias):
    index = [lax.axis_index(a).astype(jnp.int32) for a in AXES]
    batch = index[0] * 2 + index[1]
    place = jnp.stack([(batch * NZ + index[2]) * 8 + index[4], index[3], batch])
    sems = pltpu.SemaphoreType.DMA
    enc_space, dec_space = VMEM((D, LAT), bf16), VMEM((LAT, D), bf16)
    (home,) = call(
        setup_kernel,
        "setup",
        [((2 * NZ * BLOCK, WIDE), bf16)],
        [activations, dec_bias, indices],
        [HBM] * 3,
        [VMEM((2, D), bf16), VMEM((D,), f32), VMEM((2, K), jnp.int32), sems((3,))],
    )
    home = exchange(home, ("z_lo", "z_hi"), 2 * NZ)
    home = exchange(jnp.broadcast_to(home[None], (4, 2 * NZ * BLOCK, WIDE)).reshape(HOME, WIDE), "y", 4)
    *sent, onehot = call(
        route_kernel,
        "route",
        [((CHUNK, D + IDS), bf16)] * NX + [((PAIRS, 2 * HOME), bf16)],
        [place, home, swap_cores(home)],
        [SMEM, VMEM, VMEM],
    )
    xs = [sent[0]] + [step(sent[d], "x", NX, d) for d in range(1, NX)]
    *ys, codes, sel = call(
        code_kernel,
        "codes",
        [((CHUNK, D + IDS), bf16)] * NX + [((PAIRS, LAT), bf16)] * 2,
        [*xs, enc_weight, dec_weight, enc_bias.reshape(1, LAT)],
        [VMEM] * NX + [HBM, HBM, VMEM],
        [enc_space, dec_space, sems((PARTS + 1,))],
        mib=20,
    )
    ys = [ys[0]] + [step(ys[d], "x", NX, -d) for d in range(1, NX)]
    own, other = call(collect_kernel, "collect", [((HOME, QUARTER), bf16)] * 2, [*ys, onehot])
    parts = (own.astype(f32) + swap_cores(other).astype(f32)).astype(bf16)
    parts = exchange(parts, BATCH, NB)
    wide, part = call(
        add_parts_kernel, "add_parts", [((PART, QUARTER), f32), ((PART, QUARTER), bf16)], [parts]
    )
    grad, sums = call(
        residual_kernel,
        "residual",
        [((HOME, QUARTER), bf16), ((1, D + VCOLS), f32)],
        [place, wide] + [step(part, "z_hi", NZ, d) for d in range(1, NZ)] + [home],
        [SMEM] + [VMEM] * 5,
    )
    grad = exchange(grad, BATCH, NB)
    sent = call(
        dispatch_kernel,
        "dispatch",
        [((CHUNK, D), bf16)] * NX + [((CHUNK, IDS), bf16)] * NX,
        [onehot, grad, swap_cores(grad), *ys],
    )
    gs, ps = sent[:NX], sent[NX:]
    ps = [ps[0]] + [step(ps[d], "x", NX, d) for d in range(1, NX)]
    gs = [gs[0]] + [step(gs[d], "x", NX, d) for d in range(1, NX)]
    pre, grad_encbias, vec = call(
        pre_kernel,
        "pre",
        [((PAIRS, LAT), bf16), ((1, LAT), f32), ((VROWS, VCOLS), f32)],
        [*ps, enc_weight, sel, sums],
        [VMEM] * NX + [HBM, VMEM, VMEM],
        [enc_space, sems((PARTS,))],
        mib=12,
    )
    def spread(kernel, name, copies, *args):
        bound = lambda *refs: kernel(copies, *refs)
        return call(bound, name, [((copies * VROWS, VCOLS), f32)], args)[0]

    vec = spread(pair_vector_kernel, "vector_cores", 8, vec, swap_cores(vec))
    vec, gs = lax.optimization_barrier((exchange(vec, ("z_lo", "z_hi"), 8), gs))
    grad_enc, grad_dec = call(
        grads_kernel,
        "grads",
        [((D, LAT), bf16), ((LAT, D), bf16)],
        [*xs, *gs, pre, codes, dec_weight],
        [HBM] * (2 * NX + 3),
        [
            VMEM((PAIRS, D + IDS), bf16),
            VMEM((PAIRS, D), bf16),
            VMEM((PAIRS, LAT), bf16),
            VMEM((PAIRS, LAT), bf16),
            dec_space,
            sems((2 * NX + 3,)),
        ],
        mib=32,
    )
    vec = spread(vector_kernel, "vector_z", 16, vec)
    vec = exchange(vec, ("y", "x"), 16)
    vec, grad_enc, grad_dec = lax.optimization_barrier((vec, grad_enc, grad_dec))
    loss, grad_decbias = call(
        last_vector_kernel,
        "vector_yx",
        [((1, 1), f32), ((D,), f32)],
        [vec],
    )
    return loss.reshape(()), grad_enc, grad_dec, grad_encbias.reshape(LAT), grad_decbias


def solution(mesh):
    split = Mesh(mesh.devices.reshape(SIZES), AXES)
    return jax.shard_map(
        local,
        mesh=split,
        in_specs=(P(AXES, None), P(AXES, None), P(None, AXES), P(AXES, None), P(AXES), P()),
        out_specs=(P(), P(None, AXES), P(AXES, None), P(AXES), P()),
        check_vma=False,
    )
```

```python
import jax
import jax.numpy as jnp
from jax import lax
from jax.experimental import pallas as pl
from jax.experimental.pallas import tpu as pltpu
from jax.sharding import Mesh, PartitionSpec as P

bf16 = jnp.bfloat16
f32 = jnp.float32

AXES = ("y", "z_lo", "z_hi", "x", "core")
SIZES = (4, 2, 4, 4, 2)
BATCH = ("y", "z_lo")

D = 3584
QUARTER = D // 4
LAT = 384
NB = 8
NZ = 4
NX = 4
NCOL = NB * NZ
SLOTS = 4
K = 64
ENTRIES = 2 * K
IDS = 128
WIDE = D + IDS
PAIRS = 128
CHUNK = PAIRS // NX
PIECE = CHUNK // 2
BLOCK = 8
HOME = NCOL * BLOCK
PART = NZ * BLOCK
ROWS = 512
DEVICES = 256
VROWS, VCOLS = 8, 512


def dot(a, b, dims=((1,), (0,))):
    return lax.dot_general(a, b, (dims, ((), ())), preferred_element_type=f32)


def iota(shape, axis):
    return lax.broadcasted_iota(jnp.int32, shape, axis)


def quarters(row):
    return [row[:, q * QUARTER : (q + 1) * QUARTER] for q in range(4)]


def fetch(pairs, sems):
    copies = [pltpu.make_async_copy(a, b, sems.at[i]) for i, (a, b) in enumerate(pairs)]
    for c in copies:
        c.start()
    return copies


def setup_kernel(act_hbm, bias_hbm, idx_hbm, out_ref, ids_ref, act_ref, bias_ref, idx_ref, sems):
    copies = fetch([(idx_hbm, idx_ref), (act_hbm, act_ref), (bias_hbm, bias_ref)], sems)
    copies[0].wait()
    idx = jnp.concatenate([idx_ref[0:1, :], idx_ref[1:2, :]], axis=1)
    ids_ref[...] = jnp.broadcast_to(idx, ids_ref.shape)
    copies[1].wait()
    copies[2].wait()
    centred = act_ref[...].astype(f32) - bias_ref[...].reshape(1, D)
    rows = jnp.concatenate(quarters(centred[0:1]) + quarters(centred[1:2]), axis=0)
    block = jnp.concatenate([rows, rows], axis=0).astype(bf16)
    for i in range(out_ref.shape[0] // (2 * BLOCK)):
        out_ref[i * 2 * BLOCK : (i + 1) * 2 * BLOCK, :] = block


def take_rows(onehot, rows, q):
    lane = iota((1, HOME), 1)
    return dot(jnp.where(lane % 4 == q, onehot, jnp.zeros((), bf16)), rows).astype(bf16)


def prefix():
    return (iota((ENTRIES, ENTRIES), 0) <= iota((ENTRIES, ENTRIES), 1)).astype(bf16)


def owner_kernel(place_ref, ids_ref, enc_hbm, dec_hbm, bias_hbm, *refs):
    outs, (sel_ref, enc_ref, dec_ref, bias_ref, sems) = refs[: 2 * NX], refs[2 * NX :]
    copies = fetch([(bias_hbm, bias_ref), (dec_hbm, dec_ref), (enc_hbm, enc_ref)], sems)
    x, core, me = place_ref[0], place_ref[1], place_ref[3]
    number = ids_ref[...] - me * LAT
    ours = ((number >= 0) & (number < LAT)).astype(f32)
    count = dot(ours.astype(bf16), prefix())
    high, low = (number >> 7).astype(f32), (number & 127).astype(f32)
    n = DEVICES // NB
    before = jnp.zeros((n, 1), f32)
    highs = [jnp.zeros((n, ENTRIES), f32) for _ in range(SLOTS)]
    lows = [jnp.zeros((n, ENTRIES), f32) for _ in range(SLOTS)]
    for b in range(NB):
        part = slice(b * n, (b + 1) * n)
        rank = jnp.where(ours[part] > 0.5, count[part] + before, 0.0)
        before = before + count[part][:, ENTRIES - 1 :]
        for k in range(SLOTS):
            mine = rank == k + 1
            highs[k] = highs[k] + jnp.where(mine, high[part], 0.0)
            lows[k] = lows[k] + jnp.where(mine, low[part], 0.0)
    lane = iota((n, ENTRIES), 1)
    table = jnp.zeros((n, ENTRIES), f32)
    for k in range(SLOTS):
        table = table + jnp.where(lane == k, jnp.sum(highs[k], axis=1, keepdims=True), 0.0)
        table = table + jnp.where(lane == SLOTS + k, jnp.sum(lows[k], axis=1, keepdims=True), 0.0)
    pair = iota((PAIRS, n), 0)
    home_x = (x + NX - pair // CHUNK) % NX
    home_core = (core + pair // (CHUNK // 2)) % 2
    group = ((pair // SLOTS) % NZ) * 8 + home_x * 2 + home_core
    found = dot((iota((PAIRS, n), 1) == group).astype(bf16), table.astype(bf16))
    lane = iota((PAIRS, ENTRIES), 1)
    slot = iota((PAIRS, ENTRIES), 0) % SLOTS
    weight = jnp.where(lane == slot, 128.0, jnp.where(lane == SLOTS + slot, 1.0, 0.0))
    number = jnp.sum(found * weight, axis=1, keepdims=True)
    sel = (number == iota((PAIRS, LAT), 1).astype(f32)).astype(f32)
    copies[0].wait()
    bias = jnp.sum(sel * bias_ref[...].astype(f32).reshape(1, LAT), axis=1, keepdims=True)
    bias = jnp.broadcast_to(bias, (PAIRS, IDS)).astype(bf16)
    sel = sel.astype(bf16)
    sel_ref[...] = sel
    copies[1].wait()
    dec = dot(sel, dec_ref[...]).astype(bf16)
    copies[2].wait()
    enc = dot(sel, enc_ref[...], ((1,), (1,))).astype(bf16)
    for i, out in enumerate(outs):
        part = slice(i * PIECE, (i + 1) * PIECE)
        out[:, :D] = dec[part]
        out[:, D : 2 * D] = enc[part]
        out[:, 2 * D :] = bias[part]


def route_kernel(place_ref, ids_ref, onehot_ref):
    x, core, me = place_ref[0], place_ref[1], place_ref[3]
    n = NX * 2 * SLOTS
    row = iota((n, ENTRIES), 0)
    first = me - x * 2 - core + ((x + row // (2 * SLOTS)) % NX) * 2 + (core + row // SLOTS) % 2
    slot = (row % SLOTS + 1).astype(f32)
    ours = []
    for s in range(NCOL):
        number = ids_ref[pl.ds(s * 8 + x * 2 + core, 1), :] - first * LAT
        ours.append(((number >= 0) & (number < LAT)).astype(f32))
    count = dot(jnp.concatenate(ours, axis=0).astype(bf16), prefix())
    chosen = [None] * NCOL
    for z in range(NZ):
        before = jnp.zeros((n, 1), f32)
        for b in range(NB):
            at = b * NZ + z
            here = count[at * n : (at + 1) * n]
            chosen[at] = jnp.where(here + before == slot, ours[at], 0.0)
            before = before + here[:, ENTRIES - 1 :]
    lane = iota((ENTRIES, ENTRIES), 1)
    second = (iota((ENTRIES, ENTRIES), 0) // K == (lane % BLOCK) // 4).astype(bf16)
    spread = dot(jnp.concatenate(chosen, axis=0).astype(bf16), second)
    place = iota((n, ENTRIES), 1) // BLOCK
    per = ENTRIES // BLOCK
    groups = []
    for z in range(NZ):
        tiles = [jnp.zeros((n, ENTRIES), f32) for _ in range(HOME // ENTRIES)]
        for b in range(NB):
            at = b * NZ + z
            part = jnp.where(place == at % per, spread[at * n : (at + 1) * n], 0.0)
            tiles[at // per] = tiles[at // per] + part
        groups.append(jnp.concatenate(tiles, axis=1))
    to, frm = iota((PAIRS, PAIRS), 0), iota((PAIRS, PAIRS), 1)
    source = ((to // SLOTS) % NZ) * n + (to // PIECE) * SLOTS + to % SLOTS
    order = (frm == source).astype(bf16)
    onehot_ref[...] = dot(order, jnp.concatenate(groups, axis=0).astype(bf16)).astype(bf16)


def gathered(refs):
    return jnp.concatenate([r[...] for r in refs], axis=0)


def collect_kernel(*refs):
    w = gathered(refs[: 2 * NX])
    rows_ref, onehot_ref, sums_ref, code_ref = refs[2 * NX : 2 * NX + 4]
    outs = refs[2 * NX + 4 :]
    onehot = onehot_ref[...]
    home = rows_ref[...]
    code = w[:, 2 * D : 2 * D + 1].astype(f32)
    for q in range(4):
        rows = take_rows(onehot, home, q)
        for d, out in enumerate(outs):
            out[:, q * QUARTER : (q + 1) * QUARTER] = rows[d * CHUNK : (d + 1) * CHUNK]
        enc = w[:, D + q * QUARTER : D + (q + 1) * QUARTER]
        code = code + jnp.sum(rows.astype(f32) * enc.astype(f32), axis=1, keepdims=True)
    code = code.astype(bf16).astype(f32)
    code_ref[...] = jnp.broadcast_to(code, (PAIRS, IDS)).astype(bf16)
    coded = (onehot.astype(f32) * code).astype(bf16)
    lane = iota((1, HOME), 1)
    total = jnp.zeros((HOME, QUARTER), f32)
    for q in range(4):
        pick = jnp.where(lane % 4 == q, coded, jnp.zeros((), bf16))
        total = total + dot(pick, w[:, q * QUARTER : (q + 1) * QUARTER], ((0,), (0,)))
    sums_ref[...] = total.astype(bf16)


def add_parts_kernel(parts_ref, wide_ref, out_ref):
    total = parts_ref[:PART, :].astype(f32)
    for b in range(1, NB):
        total = total + parts_ref[b * PART : (b + 1) * PART, :].astype(f32)
    wide_ref[...] = total
    out_ref[...] = total.astype(bf16)


def residual_kernel(place_ref, wide_ref, p1, p2, p3, home_ref, out_ref, sums_ref):
    rebuilt = wide_ref[...] + (p1[...].astype(f32) + p2[...].astype(f32) + p3[...].astype(f32))
    first = pl.multiple_of(place_ref[2] * PART, PART)
    residual = rebuilt - home_ref[pl.ds(first, PART), :].astype(f32)
    grad = residual.astype(bf16)
    for b in range(NB):
        out_ref[b * PART : (b + 1) * PART, :] = grad
    columns = jnp.sum(residual.reshape(NZ, BLOCK, QUARTER), axis=0) * (1.0 / NZ)
    for q in range(4):
        sums_ref[:, q * QUARTER : (q + 1) * QUARTER] = columns[q : q + 1] + columns[q + 4 : q + 5]
    square = jnp.sum(residual * residual) * (1.0 / (NZ * ROWS * D))
    sums_ref[:, D:] = jnp.full((1, VCOLS), square, f32)


def pre_kernel(onehot_ref, grad_ref, sums_ref, *refs):
    w = gathered(refs[: 2 * NX])
    pre_ref, vec_ref = refs[2 * NX :]
    onehot = onehot_ref[...]
    grad = grad_ref[...]
    pre = jnp.zeros((PAIRS, 1), f32)
    for q in range(4):
        rows = take_rows(onehot, grad, q)
        dec = w[:, q * QUARTER : (q + 1) * QUARTER]
        pre = pre + jnp.sum(rows.astype(f32) * dec.astype(f32), axis=1, keepdims=True)
    pre = jnp.broadcast_to(pre, (PAIRS, IDS)).astype(bf16)
    pre_ref[...] = pre
    term = dot(pre, w[:, D : 2 * D], ((0,), (0,)))
    vec = sums_ref[:, :D] - term[0:1]
    for i in range(VROWS - 1):
        vec_ref[i : i + 1, :] = vec[:, i * VCOLS : (i + 1) * VCOLS]
    vec_ref[VROWS - 1 :, :] = sums_ref[:, D:]


def dispatch_kernel(onehot_ref, grad_ref, code_ref, pre_ref, g0, g1, g2, g3):
    onehot = onehot_ref[...]
    grad = grad_ref[...]
    for q in range(4):
        rows = take_rows(onehot, grad, q)
        for d, out in enumerate((g0, g1, g2, g3)):
            out[:, q * QUARTER : (q + 1) * QUARTER] = rows[d * CHUNK : (d + 1) * CHUNK]
    scalars = jnp.where(iota((PAIRS, IDS), 1) == 0, code_ref[...], pre_ref[...])
    for d, out in enumerate((g0, g1, g2, g3)):
        out[:, D:] = scalars[d * CHUNK : (d + 1) * CHUNK]


def grads_kernel(x0, x1, x2, x3, xs_hbm, dec_hbm, g0, g1, g2, g3, gs_ref, sel_ref, genc_ref, gdec_ref, bias_ref, x_ref, dec_ref, sems):
    pairs = [(dec_hbm, dec_ref)]
    parts = []
    for d, (x, g) in enumerate(((x0, g0), (x1, g1), (x2, g2), (x3, g3))):
        mine, theirs = pl.ds(d * CHUNK, PIECE), pl.ds(d * CHUNK + PIECE, PIECE)
        here = pl.ds(d * PIECE, PIECE)
        pairs.append((x.at[pl.ds(0, PIECE)], x_ref.at[mine]))
        pairs.append((xs_hbm.at[here], x_ref.at[theirs]))
        parts += [g[:PIECE, :], gs_ref[here, :]]
    copies = fetch(pairs, sems)
    g = jnp.concatenate(parts, axis=0)
    sel = sel_ref[...].astype(f32)
    pre = sel * g[:, D + 1 : D + 2].astype(f32)
    bias_ref[...] = jnp.sum(pre, axis=0)
    codes = (sel * g[:, D : D + 1].astype(f32)).astype(bf16)
    raw = dot(codes, g[:, :D], ((0,), (0,)))
    copies[0].wait()
    dec = dec_ref[...].astype(f32)
    along = jnp.sum(raw * dec, axis=1, keepdims=True)
    norm = jnp.sum(dec * dec, axis=1, keepdims=True)
    gdec_ref[...] = (raw - (along / (norm + 1e-06)) * dec).astype(bf16)
    for c in copies[1:]:
        c.wait()
    genc_ref[...] = dot(x_ref[...], pre.astype(bf16), ((0,), (0,))).astype(bf16)


def vector_kernel(copies, parts_ref, out_ref):
    total = parts_ref[:VROWS, :]
    for i in range(1, parts_ref.shape[0] // VROWS):
        total = total + parts_ref[i * VROWS : (i + 1) * VROWS, :]
    for i in range(copies):
        out_ref[i * VROWS : (i + 1) * VROWS, :] = total


def last_vector_kernel(parts_ref, loss_ref, out_ref):
    total = parts_ref[:VROWS, :]
    for i in range(1, parts_ref.shape[0] // VROWS):
        total = total + parts_ref[i * VROWS : (i + 1) * VROWS, :]
    for i in range(VROWS - 1):
        out_ref[pl.ds(i * VCOLS, VCOLS)] = total[i : i + 1, :].reshape(VCOLS)
    loss_ref[...] = total[VROWS - 1 :, :1]


def pair_vector_kernel(copies, own_ref, other_ref, out_ref):
    total = own_ref[...] + other_ref[...]
    for i in range(copies):
        out_ref[i * VROWS : (i + 1) * VROWS, :] = total


SMEM, VMEM, HBM = pltpu.SMEM, pltpu.VMEM, pltpu.HBM


def call(kernel, name, outs, args, spaces=None, scratch=(), mib=8):
    spaces = spaces or [VMEM] * len(args)
    args = [
        pltpu.with_memory_space_constraint(a, HBM) if s is HBM else a for a, s in zip(args, spaces)
    ]
    return pl.pallas_call(
        kernel,
        out_shape=[HBM(o[0], o[1]) if len(o) > 2 else jax.ShapeDtypeStruct(*o) for o in outs],
        in_specs=[pl.BlockSpec(memory_space=s) for s in spaces],
        out_specs=[pl.BlockSpec(memory_space=VMEM) for _ in outs],
        scratch_shapes=list(scratch),
        compiler_params=pltpu.CompilerParams(vmem_limit_bytes=mib * 1024 * 1024),
        name=name,
    )(*args)


def exchange(x, axes, peers):
    shape = x.shape
    x = x.reshape(peers, shape[0] // peers, shape[1])
    return lax.all_to_all(x, axes, split_axis=0, concat_axis=0).reshape(shape)


def step(x, axis, size, by):
    return lax.ppermute(x, axis, [(i, (i + by) % size) for i in range(size)])


def swap_cores(x):
    return step(x, "core", 2, 1)


def hop(chunks, way):
    return [chunks[0]] + [step(chunks[d], "x", NX, way * d) for d in range(1, NX)]


def swap_halves(chunks):
    return swap_cores(jnp.concatenate([c[PIECE:] for c in chunks]))


def to_homes(pieces):
    out = [pieces[0]]
    for i in range(1, 2 * NX):
        by_x, by_core = i // 2, i % 2
        way = [(x * 2 + c, (x - by_x) % NX * 2 + (c + by_core) % 2) for x in range(NX) for c in range(2)]
        out.append(lax.ppermute(pieces[i], ("x", "core"), way))
    return out


def local(activations, indices, enc_weight, dec_weight, enc_bias, dec_bias):
    index = [lax.axis_index(a).astype(jnp.int32) for a in AXES]
    batch = index[0] * 2 + index[1]
    me = (batch * NZ + index[2]) * 8 + index[3] * 2 + index[4]
    place = jnp.stack([index[3], index[4], batch, me])
    sems = pltpu.SemaphoreType.DMA
    enc_space, dec_space = VMEM((D, LAT), bf16), VMEM((LAT, D), bf16)
    home, ids = call(
        setup_kernel,
        "setup",
        [((HOME, QUARTER), bf16), ((DEVICES, ENTRIES), jnp.int32)],
        [activations, dec_bias, indices],
        [HBM] * 3,
        [VMEM((2, D), bf16), VMEM((D,), f32), VMEM((2, K), jnp.int32), sems((3,))],
    )
    ids = exchange(ids, AXES, DEVICES)
    *ws, sel = call(
        owner_kernel,
        "owner",
        [((PIECE, 2 * D + IDS), bf16)] * (2 * NX) + [((PAIRS, LAT), bf16)],
        [place, ids, enc_weight, dec_weight, enc_bias],
        [SMEM, VMEM, HBM, HBM, HBM],
        [enc_space, dec_space, VMEM((LAT,), bf16), sems((3,))],
        mib=20,
    )
    (onehot,) = call(route_kernel, "route", [((PAIRS, HOME), bf16)], [place, ids], [SMEM, VMEM])
    home, _ = lax.optimization_barrier((home, sel))
    home = exchange(home, AXES[:3], NCOL)
    ws = to_homes(ws)
    parts, code, *xs = call(
        collect_kernel,
        "collect",
        [((HOME, QUARTER), bf16), ((PAIRS, IDS), bf16)] + [((CHUNK, D), bf16, HBM)] * NX,
        [*ws, home, onehot],
        mib=12,
    )
    xs = hop(xs, 1)
    parts, xs[2] = lax.optimization_barrier((exchange(parts, BATCH, NB), xs[2]))
    wide, part = call(
        add_parts_kernel, "add_parts", [((PART, QUARTER), f32), ((PART, QUARTER), bf16)], [parts]
    )
    grad, sums = call(
        residual_kernel,
        "residual",
        [((HOME, QUARTER), bf16), ((1, D + VCOLS), f32)],
        [place, wide] + [step(part, "z_hi", NZ, d) for d in range(1, NZ)] + [home],
        [SMEM] + [VMEM] * 5,
    )
    grad, xs[1], xs[3] = lax.optimization_barrier((exchange(grad, BATCH, NB), xs[1], xs[3]))
    pre, vec = call(
        pre_kernel,
        "pre",
        [((PAIRS, IDS), bf16), ((VROWS, VCOLS), f32)],
        [onehot, grad, sums, *ws],
        mib=12,
    )
    gs = call(
        dispatch_kernel,
        "dispatch",
        [((CHUNK, WIDE), bf16)] * NX,
        [onehot, grad, code, pre],
    )
    gs = hop(gs, 1)

    def spread(kernel, name, copies, *args):
        bound = lambda *refs: kernel(copies, *refs)
        return call(bound, name, [((copies * VROWS, VCOLS), f32)], args)[0]

    vec = spread(pair_vector_kernel, "vector_cores", 8, vec, swap_cores(vec))
    vec, gs = lax.optimization_barrier((exchange(vec, ("z_lo", "z_hi"), 8), gs))
    grad_enc, grad_dec, grad_encbias = call(
        grads_kernel,
        "grads",
        [((D, LAT), bf16), ((LAT, D), bf16), ((LAT,), f32)],
        [*xs, swap_halves(xs), dec_weight, *gs, swap_halves(gs), sel],
        [HBM] * (NX + 2) + [VMEM] * (NX + 2),
        [VMEM((PAIRS, D), bf16), dec_space, sems((2 * NX + 1,))],
        mib=32,
    )
    vec = spread(vector_kernel, "vector_z", 16, vec)
    vec = exchange(vec, ("y", "x"), 16)
    vec, grad_enc, grad_dec = lax.optimization_barrier((vec, grad_enc, grad_dec))
    loss, grad_decbias = call(
        last_vector_kernel,
        "vector_yx",
        [((1, 1), f32), ((D,), f32)],
        [vec],
    )
    return loss.reshape(()), grad_enc, grad_dec, grad_encbias, grad_decbias


def solution(mesh):
    split = Mesh(mesh.devices.reshape(SIZES), AXES)
    return jax.shard_map(
        local,
        mesh=split,
        in_specs=(P(AXES, None), P(AXES, None), P(None, AXES), P(AXES, None), P(AXES), P()),
        out_specs=(P(), P(None, AXES), P(AXES, None), P(AXES), P()),
        check_vma=False,
    )
```

```python
import jax
import jax.numpy as jnp
from jax import lax
from jax.experimental import pallas as pl
from jax.experimental.pallas import tpu as pltpu
from jax.sharding import Mesh, PartitionSpec as P

bf16 = jnp.bfloat16
f32 = jnp.float32

AXES = ("y", "z_lo", "z_hi", "x", "core")
SIZES = (4, 2, 4, 4, 2)
BATCH = ("y", "z_lo")

D = 3584
QUARTER = D // 4
LAT = 384
NB = 8
NZ = 4
NX = 4
NCOL = NB * NZ
SLOTS = 4
K = 64
ENTRIES = 2 * K
IDS = 128
WIDE = D + IDS
PAIRS = 128
CHUNK = PAIRS // NX
PIECE = CHUNK // 2
BLOCK = 8
HOME = NCOL * BLOCK
PART = NZ * BLOCK
ROWS = 512
DEVICES = 256
VROWS, VCOLS = 8, 512


def dot(a, b, dims=((1,), (0,))):
    return lax.dot_general(a, b, (dims, ((), ())), preferred_element_type=f32)


def iota(shape, axis):
    return lax.broadcasted_iota(jnp.int32, shape, axis)


def quarters(row):
    return [row[:, q * QUARTER : (q + 1) * QUARTER] for q in range(4)]


def fetch(pairs, sems):
    copies = [pltpu.make_async_copy(a, b, sems.at[i]) for i, (a, b) in enumerate(pairs)]
    for c in copies:
        c.start()
    return copies


def setup_kernel(act_hbm, bias_hbm, idx_hbm, out_ref, ids_ref, act_ref, bias_ref, idx_ref, sems):
    copies = fetch([(idx_hbm, idx_ref), (act_hbm, act_ref), (bias_hbm, bias_ref)], sems)
    copies[0].wait()
    idx = jnp.concatenate([idx_ref[0:1, :], idx_ref[1:2, :]], axis=1)
    ids_ref[...] = jnp.broadcast_to(idx, ids_ref.shape)
    copies[1].wait()
    copies[2].wait()
    centred = act_ref[...].astype(f32) - bias_ref[...].reshape(1, D)
    rows = jnp.concatenate(quarters(centred[0:1]) + quarters(centred[1:2]), axis=0)
    block = jnp.concatenate([rows, rows], axis=0).astype(bf16)
    for i in range(out_ref.shape[0] // (2 * BLOCK)):
        out_ref[i * 2 * BLOCK : (i + 1) * 2 * BLOCK, :] = block


def take_rows(onehot, rows, q):
    lane = iota((1, HOME), 1)
    return dot(jnp.where(lane % 4 == q, onehot, jnp.zeros((), bf16)), rows).astype(bf16)


def prefix():
    return (iota((ENTRIES, ENTRIES), 0) <= iota((ENTRIES, ENTRIES), 1)).astype(bf16)


def owner_kernel(place_ref, ids_ref, enc_hbm, dec_hbm, bias_hbm, *refs):
    outs, (sel_ref, enc_ref, dec_ref, bias_ref, sems) = refs[: 2 * NX], refs[2 * NX :]
    copies = fetch([(bias_hbm, bias_ref), (dec_hbm, dec_ref), (enc_hbm, enc_ref)], sems)
    x, core, me = place_ref[0], place_ref[1], place_ref[3]
    number = ids_ref[...] - me * LAT
    ours = ((number >= 0) & (number < LAT)).astype(f32)
    count = dot(ours.astype(bf16), prefix())
    high, low = (number >> 7).astype(f32), (number & 127).astype(f32)
    n = DEVICES // NB
    before = jnp.zeros((n, 1), f32)
    highs = [jnp.zeros((n, ENTRIES), f32) for _ in range(SLOTS)]
    lows = [jnp.zeros((n, ENTRIES), f32) for _ in range(SLOTS)]
    for b in range(NB):
        part = slice(b * n, (b + 1) * n)
        rank = jnp.where(ours[part] > 0.5, count[part] + before, 0.0)
        before = before + count[part][:, ENTRIES - 1 :]
        for k in range(SLOTS):
            mine = rank == k + 1
            highs[k] = highs[k] + jnp.where(mine, high[part], 0.0)
            lows[k] = lows[k] + jnp.where(mine, low[part], 0.0)
    lane = iota((n, ENTRIES), 1)
    table = jnp.zeros((n, ENTRIES), f32)
    for k in range(SLOTS):
        table = table + jnp.where(lane == k, jnp.sum(highs[k], axis=1, keepdims=True), 0.0)
        table = table + jnp.where(lane == SLOTS + k, jnp.sum(lows[k], axis=1, keepdims=True), 0.0)
    pair = iota((PAIRS, n), 0)
    home_x = (x + NX - pair // CHUNK) % NX
    home_core = (core + pair // (CHUNK // 2)) % 2
    group = ((pair // SLOTS) % NZ) * 8 + home_x * 2 + home_core
    found = dot((iota((PAIRS, n), 1) == group).astype(bf16), table.astype(bf16))
    lane = iota((PAIRS, ENTRIES), 1)
    slot = iota((PAIRS, ENTRIES), 0) % SLOTS
    weight = jnp.where(lane == slot, 128.0, jnp.where(lane == SLOTS + slot, 1.0, 0.0))
    number = jnp.sum(found * weight, axis=1, keepdims=True)
    sel = (number == iota((PAIRS, LAT), 1).astype(f32)).astype(f32)
    copies[0].wait()
    bias = jnp.sum(sel * bias_ref[...].astype(f32).reshape(1, LAT), axis=1, keepdims=True)
    bias = jnp.broadcast_to(bias, (PAIRS, IDS)).astype(bf16)
    sel = sel.astype(bf16)
    sel_ref[...] = sel
    copies[1].wait()
    dec = dot(sel, dec_ref[...]).astype(bf16)
    copies[2].wait()
    enc = dot(sel, enc_ref[...], ((1,), (1,))).astype(bf16)
    for i, out in enumerate(outs):
        part = slice(i * PIECE, (i + 1) * PIECE)
        out[:, :D] = dec[part]
        out[:, D : 2 * D] = enc[part]
        out[:, 2 * D :] = bias[part]


def route_kernel(place_ref, ids_ref, onehot_ref):
    x, core, me = place_ref[0], place_ref[1], place_ref[3]
    n = NX * 2 * SLOTS
    row = iota((n, ENTRIES), 0)
    first = me - x * 2 - core + ((x + row // (2 * SLOTS)) % NX) * 2 + (core + row // SLOTS) % 2
    slot = (row % SLOTS + 1).astype(f32)
    ours = []
    for s in range(NCOL):
        number = ids_ref[pl.ds(s * 8 + x * 2 + core, 1), :] - first * LAT
        ours.append(((number >= 0) & (number < LAT)).astype(f32))
    count = dot(jnp.concatenate(ours, axis=0).astype(bf16), prefix())
    chosen = [None] * NCOL
    for z in range(NZ):
        before = jnp.zeros((n, 1), f32)
        for b in range(NB):
            at = b * NZ + z
            here = count[at * n : (at + 1) * n]
            chosen[at] = jnp.where(here + before == slot, ours[at], 0.0)
            before = before + here[:, ENTRIES - 1 :]
    lane = iota((ENTRIES, ENTRIES), 1)
    second = (iota((ENTRIES, ENTRIES), 0) // K == (lane % BLOCK) // 4).astype(bf16)
    spread = dot(jnp.concatenate(chosen, axis=0).astype(bf16), second)
    place = iota((n, ENTRIES), 1) // BLOCK
    per = ENTRIES // BLOCK
    groups = []
    for z in range(NZ):
        tiles = [jnp.zeros((n, ENTRIES), f32) for _ in range(HOME // ENTRIES)]
        for b in range(NB):
            at = b * NZ + z
            part = jnp.where(place == at % per, spread[at * n : (at + 1) * n], 0.0)
            tiles[at // per] = tiles[at // per] + part
        groups.append(jnp.concatenate(tiles, axis=1))
    to, frm = iota((PAIRS, PAIRS), 0), iota((PAIRS, PAIRS), 1)
    source = ((to // SLOTS) % NZ) * n + (to // PIECE) * SLOTS + to % SLOTS
    order = (frm == source).astype(bf16)
    onehot_ref[...] = dot(order, jnp.concatenate(groups, axis=0).astype(bf16)).astype(bf16)


ORDER = ((3, 0), (1, 0), (2, 0), (2, 1), (3, 1), (1, 1), (0, 1), (0, 0))
X_ORDER = (2, 1, 3, 0)


def gathered(refs):
    at = [ORDER.index((i // 2, i % 2)) for i in range(2 * NX)]
    return jnp.concatenate([refs[i][...] for i in at], axis=0)


def in_order(chunks):
    return [chunks[d] for d in X_ORDER]


def collect_kernel(*refs):
    w = gathered(refs[: 2 * NX])
    rows_ref, onehot_ref, sums_ref, code_ref = refs[2 * NX : 2 * NX + 4]
    outs = refs[2 * NX + 4 :]
    onehot = onehot_ref[...]
    home = rows_ref[...]
    code = w[:, 2 * D : 2 * D + 1].astype(f32)
    for q in range(4):
        rows = take_rows(onehot, home, q)
        for d, out in enumerate(outs):
            out[:, q * QUARTER : (q + 1) * QUARTER] = rows[d * CHUNK : (d + 1) * CHUNK]
        enc = w[:, D + q * QUARTER : D + (q + 1) * QUARTER]
        code = code + jnp.sum(rows.astype(f32) * enc.astype(f32), axis=1, keepdims=True)
    code = code.astype(bf16).astype(f32)
    code_ref[...] = jnp.broadcast_to(code, (PAIRS, IDS)).astype(bf16)
    coded = (onehot.astype(f32) * code).astype(bf16)
    lane = iota((1, HOME), 1)
    total = jnp.zeros((HOME, QUARTER), f32)
    for q in range(4):
        pick = jnp.where(lane % 4 == q, coded, jnp.zeros((), bf16))
        total = total + dot(pick, w[:, q * QUARTER : (q + 1) * QUARTER], ((0,), (0,)))
    sums_ref[...] = total.astype(bf16)


def add_parts_kernel(parts_ref, wide_ref, out_ref):
    total = parts_ref[:PART, :].astype(f32)
    for b in range(1, NB):
        total = total + parts_ref[b * PART : (b + 1) * PART, :].astype(f32)
    wide_ref[...] = total
    out_ref[...] = total.astype(bf16)


def residual_kernel(place_ref, wide_ref, p1, p2, p3, home_ref, out_ref, sums_ref):
    rebuilt = wide_ref[...] + (p1[...].astype(f32) + p2[...].astype(f32) + p3[...].astype(f32))
    first = pl.multiple_of(place_ref[2] * PART, PART)
    residual = rebuilt - home_ref[pl.ds(first, PART), :].astype(f32)
    grad = residual.astype(bf16)
    for b in range(NB):
        out_ref[b * PART : (b + 1) * PART, :] = grad
    columns = jnp.sum(residual.reshape(NZ, BLOCK, QUARTER), axis=0) * (1.0 / NZ)
    for q in range(4):
        sums_ref[:, q * QUARTER : (q + 1) * QUARTER] = columns[q : q + 1] + columns[q + 4 : q + 5]
    square = jnp.sum(residual * residual) * (1.0 / (NZ * ROWS * D))
    sums_ref[:, D:] = jnp.full((1, VCOLS), square, f32)


def pre_kernel(onehot_ref, grad_ref, sums_ref, *refs):
    w = gathered(refs[: 2 * NX])
    pre_ref, vec_ref = refs[2 * NX :]
    onehot = onehot_ref[...]
    grad = grad_ref[...]
    pre = jnp.zeros((PAIRS, 1), f32)
    for q in range(4):
        rows = take_rows(onehot, grad, q)
        dec = w[:, q * QUARTER : (q + 1) * QUARTER]
        pre = pre + jnp.sum(rows.astype(f32) * dec.astype(f32), axis=1, keepdims=True)
    pre = jnp.broadcast_to(pre, (PAIRS, IDS)).astype(bf16)
    pre_ref[...] = pre
    term = dot(pre, w[:, D : 2 * D], ((0,), (0,)))
    vec = sums_ref[:, :D] - term[0:1]
    for i in range(VROWS - 1):
        vec_ref[i : i + 1, :] = vec[:, i * VCOLS : (i + 1) * VCOLS]
    vec_ref[VROWS - 1 :, :] = sums_ref[:, D:]


def dispatch_kernel(onehot_ref, grad_ref, code_ref, pre_ref, g0, g1, g2, g3):
    onehot = onehot_ref[...]
    grad = grad_ref[...]
    for q in range(4):
        rows = take_rows(onehot, grad, q)
        for d, out in enumerate((g0, g1, g2, g3)):
            out[:, q * QUARTER : (q + 1) * QUARTER] = rows[d * CHUNK : (d + 1) * CHUNK]
    scalars = jnp.where(iota((PAIRS, IDS), 1) == 0, code_ref[...], pre_ref[...])
    for d, out in enumerate((g0, g1, g2, g3)):
        out[:, D:] = scalars[d * CHUNK : (d + 1) * CHUNK]


def grads_kernel(*refs):
    xs, xs_hbm, dec_hbm = refs[:NX], refs[NX], refs[NX + 1]
    gs, gs_ref, sel_ref = refs[NX + 2 : 2 * NX + 2], refs[2 * NX + 2], refs[2 * NX + 3]
    genc_ref, gdec_ref, bias_ref, x_ref, dec_ref, sems = refs[2 * NX + 4 :]
    pairs = [(dec_hbm, dec_ref)]
    parts = []
    for d in range(NX):
        x, g = xs[X_ORDER.index(d)], gs[X_ORDER.index(d)]
        mine, theirs = pl.ds(d * CHUNK, PIECE), pl.ds(d * CHUNK + PIECE, PIECE)
        here = pl.ds(d * PIECE, PIECE)
        pairs.append((x.at[pl.ds(0, PIECE)], x_ref.at[mine]))
        pairs.append((xs_hbm.at[here], x_ref.at[theirs]))
        parts += [g[:PIECE, :], gs_ref[here, :]]
    copies = fetch(pairs, sems)
    g = jnp.concatenate(parts, axis=0)
    sel = sel_ref[...].astype(f32)
    pre = sel * g[:, D + 1 : D + 2].astype(f32)
    bias_ref[...] = jnp.sum(pre, axis=0)
    codes = (sel * g[:, D : D + 1].astype(f32)).astype(bf16)
    raw = dot(codes, g[:, :D], ((0,), (0,)))
    copies[0].wait()
    dec = dec_ref[...].astype(f32)
    along = jnp.sum(raw * dec, axis=1, keepdims=True)
    norm = jnp.sum(dec * dec, axis=1, keepdims=True)
    gdec_ref[...] = (raw - (along / (norm + 1e-06)) * dec).astype(bf16)
    for c in copies[1:]:
        c.wait()
    genc_ref[...] = dot(x_ref[...], pre.astype(bf16), ((0,), (0,))).astype(bf16)


def vector_kernel(copies, parts_ref, out_ref):
    total = parts_ref[:VROWS, :]
    for i in range(1, parts_ref.shape[0] // VROWS):
        total = total + parts_ref[i * VROWS : (i + 1) * VROWS, :]
    for i in range(copies):
        out_ref[i * VROWS : (i + 1) * VROWS, :] = total


def last_vector_kernel(parts_ref, loss_ref, out_ref):
    total = parts_ref[:VROWS, :]
    for i in range(1, parts_ref.shape[0] // VROWS):
        total = total + parts_ref[i * VROWS : (i + 1) * VROWS, :]
    for i in range(VROWS - 1):
        out_ref[pl.ds(i * VCOLS, VCOLS)] = total[i : i + 1, :].reshape(VCOLS)
    loss_ref[...] = total[VROWS - 1 :, :1]


def pair_vector_kernel(copies, own_ref, other_ref, out_ref):
    total = own_ref[...] + other_ref[...]
    for i in range(copies):
        out_ref[i * VROWS : (i + 1) * VROWS, :] = total


SMEM, VMEM, HBM = pltpu.SMEM, pltpu.VMEM, pltpu.HBM


def call(kernel, name, outs, args, spaces=None, scratch=(), mib=8, flops=None):
    spaces = spaces or [VMEM] * len(args)
    args = [
        pltpu.with_memory_space_constraint(a, HBM) if s is HBM else a for a, s in zip(args, spaces)
    ]
    return pl.pallas_call(
        kernel,
        out_shape=[HBM(o[0], o[1]) if len(o) > 2 else jax.ShapeDtypeStruct(*o) for o in outs],
        in_specs=[pl.BlockSpec(memory_space=s) for s in spaces],
        out_specs=[pl.BlockSpec(memory_space=VMEM) for _ in outs],
        scratch_shapes=list(scratch),
        compiler_params=pltpu.CompilerParams(vmem_limit_bytes=mib * 1024 * 1024),
        name=name,
        cost_estimate=flops and pl.CostEstimate(flops=flops, bytes_accessed=0, transcendentals=0),
    )(*args)


def exchange(x, axes, peers):
    shape = x.shape
    x = x.reshape(peers, shape[0] // peers, shape[1])
    return lax.all_to_all(x, axes, split_axis=0, concat_axis=0).reshape(shape)


def step(x, axis, size, by):
    return lax.ppermute(x, axis, [(i, (i + by) % size) for i in range(size)])


def swap_cores(x):
    return step(x, "core", 2, 1)


def hop(chunks, way):
    out = list(chunks)
    for d in (2, 1, 3):
        out[d] = step(chunks[d], "x", NX, way * d)
    return out


def swap_halves(chunks):
    return swap_cores(jnp.concatenate([c[PIECE:] for c in chunks]))


def to_homes(pieces):
    out = []
    for by_x, by_core in ORDER:
        way = [(x * 2 + c, (x - by_x) % NX * 2 + (c + by_core) % 2) for x in range(NX) for c in range(2)]
        piece = pieces[by_x * 2 + by_core]
        out.append(lax.ppermute(piece, ("x", "core"), way) if by_x or by_core else piece)
    return out


def local(activations, indices, enc_weight, dec_weight, enc_bias, dec_bias):
    index = [lax.axis_index(a).astype(jnp.int32) for a in AXES]
    batch = index[0] * 2 + index[1]
    me = (batch * NZ + index[2]) * 8 + index[3] * 2 + index[4]
    place = jnp.stack([index[3], index[4], batch, me])
    sems = pltpu.SemaphoreType.DMA
    enc_space, dec_space = VMEM((D, LAT), bf16), VMEM((LAT, D), bf16)
    home, ids = call(
        setup_kernel,
        "setup",
        [((HOME, QUARTER), bf16), ((DEVICES, ENTRIES), jnp.int32)],
        [activations, dec_bias, indices],
        [HBM] * 3,
        [VMEM((2, D), bf16), VMEM((D,), f32), VMEM((2, K), jnp.int32), sems((3,))],
    )
    ids = exchange(ids, AXES, DEVICES)
    *ws, sel = call(
        owner_kernel,
        "owner",
        [((PIECE, 2 * D + IDS), bf16)] * (2 * NX) + [((PAIRS, LAT), bf16)],
        [place, ids, enc_weight, dec_weight, enc_bias],
        [SMEM, VMEM, HBM, HBM, HBM],
        [enc_space, dec_space, VMEM((LAT,), bf16), sems((3,))],
        mib=20,
    )
    (onehot,) = call(route_kernel, "route", [((PAIRS, HOME), bf16)], [place, ids], [SMEM, VMEM], flops=10**11)
    home, _ = lax.optimization_barrier((home, sel))
    home = exchange(home, AXES[:3], NCOL)
    ws = to_homes(ws)
    parts, code, *xs = call(
        collect_kernel,
        "collect",
        [((HOME, QUARTER), bf16), ((PAIRS, IDS), bf16)] + [((CHUNK, D), bf16, HBM)] * NX,
        [*ws, home, onehot],
        mib=12,
    )
    xs = hop(xs, 1)
    parts, xs[2] = lax.optimization_barrier((exchange(parts, BATCH, NB), xs[2]))
    wide, part = call(
        add_parts_kernel, "add_parts", [((PART, QUARTER), f32), ((PART, QUARTER), bf16)], [parts]
    )
    grad, sums = call(
        residual_kernel,
        "residual",
        [((HOME, QUARTER), bf16), ((1, D + VCOLS), f32)],
        [place, wide] + [step(part, "z_hi", NZ, d) for d in range(1, NZ)] + [home],
        [SMEM] + [VMEM] * 5,
    )
    grad, xs[1], xs[3] = lax.optimization_barrier((exchange(grad, BATCH, NB), xs[1], xs[3]))
    pre, vec = call(
        pre_kernel,
        "pre",
        [((PAIRS, IDS), bf16), ((VROWS, VCOLS), f32)],
        [onehot, grad, sums, *ws],
        mib=12,
    )
    gs = call(
        dispatch_kernel,
        "dispatch",
        [((CHUNK, WIDE), bf16)] * NX,
        [onehot, grad, code, pre],
    )
    gs = hop(gs, 1)

    def spread(kernel, name, copies, *args):
        bound = lambda *refs: kernel(copies, *refs)
        return call(bound, name, [((copies * VROWS, VCOLS), f32)], args)[0]

    vec = spread(pair_vector_kernel, "vector_cores", 8, vec, swap_cores(vec))
    vec, gs = lax.optimization_barrier((exchange(vec, ("z_lo", "z_hi"), 8), gs))
    grad_enc, grad_dec, grad_encbias = call(
        grads_kernel,
        "grads",
        [((D, LAT), bf16), ((LAT, D), bf16), ((LAT,), f32)],
        [*in_order(xs), swap_halves(xs), dec_weight, *in_order(gs), swap_halves(gs), sel],
        [HBM] * (NX + 2) + [VMEM] * (NX + 2),
        [VMEM((PAIRS, D), bf16), dec_space, sems((2 * NX + 1,))],
        mib=32,
    )
    vec = spread(vector_kernel, "vector_z", 16, vec)
    vec = exchange(vec, ("y", "x"), 16)
    vec, grad_enc, grad_dec = lax.optimization_barrier((vec, grad_enc, grad_dec))
    loss, grad_decbias = call(
        last_vector_kernel,
        "vector_yx",
        [((1, 1), f32), ((D,), f32)],
        [vec],
    )
    return loss.reshape(()), grad_enc, grad_dec, grad_encbias, grad_decbias


def solution(mesh):
    split = Mesh(mesh.devices.reshape(SIZES), AXES)
    return jax.shard_map(
        local,
        mesh=split,
        in_specs=(P(AXES, None), P(AXES, None), P(None, AXES), P(AXES, None), P(AXES), P()),
        out_specs=(P(), P(None, AXES), P(AXES, None), P(AXES), P()),
        check_vma=False,
    )
```

```python
import jax
import jax.numpy as jnp
from jax import lax
from jax.experimental import pallas as pl
from jax.experimental.pallas import tpu as pltpu
from jax.sharding import Mesh, PartitionSpec as P

bf16 = jnp.bfloat16
f32 = jnp.float32

AXES = ("y", "z_lo", "z_hi", "x", "core")
SIZES = (4, 2, 4, 4, 2)
BATCH = ("y", "z_lo")

D = 3584
QUARTER = D // 4
LAT = 384
NB = 8
NZ = 4
NX = 4
NCOL = NB * NZ
SLOTS = 4
K = 64
ENTRIES = 2 * K
IDS = 128
WIDE = D + IDS
PAIRS = 128
CHUNK = PAIRS // NX
PIECE = CHUNK // 2
BLOCK = 8
HOME = NCOL * BLOCK
PART = NZ * BLOCK
ROWS = 512
DEVICES = 256
VROWS, VCOLS = 8, 512


def dot(a, b, dims=((1,), (0,))):
    return lax.dot_general(a, b, (dims, ((), ())), preferred_element_type=f32)


def iota(shape, axis):
    return lax.broadcasted_iota(jnp.int32, shape, axis)


def quarters(row):
    return [row[:, q * QUARTER : (q + 1) * QUARTER] for q in range(4)]


def fetch(pairs, sems):
    copies = [pltpu.make_async_copy(a, b, sems.at[i]) for i, (a, b) in enumerate(pairs)]
    for c in copies:
        c.start()
    return copies


def setup_kernel(act_hbm, bias_hbm, idx_hbm, out_ref, ids_ref, act_ref, bias_ref, idx_ref, sems):
    copies = fetch([(idx_hbm, idx_ref), (act_hbm, act_ref), (bias_hbm, bias_ref)], sems)
    copies[0].wait()
    idx = jnp.concatenate([idx_ref[0:1, :], idx_ref[1:2, :]], axis=1)
    ids_ref[...] = jnp.broadcast_to(idx, ids_ref.shape)
    copies[1].wait()
    copies[2].wait()
    centred = act_ref[...].astype(f32) - bias_ref[...].reshape(1, D)
    rows = jnp.concatenate(quarters(centred[0:1]) + quarters(centred[1:2]), axis=0)
    block = jnp.concatenate([rows, rows], axis=0).astype(bf16)
    for i in range(out_ref.shape[0] // (2 * BLOCK)):
        out_ref[i * 2 * BLOCK : (i + 1) * 2 * BLOCK, :] = block


def take_rows(onehot, rows, q):
    lane = iota((1, HOME), 1)
    return dot(jnp.where(lane % 4 == q, onehot, jnp.zeros((), bf16)), rows).astype(bf16)


def prefix():
    return (iota((ENTRIES, ENTRIES), 0) <= iota((ENTRIES, ENTRIES), 1)).astype(bf16)


def owner_kernel(place_ref, ids_ref, enc_hbm, dec_hbm, bias_hbm, *refs):
    outs, (sel_ref, enc_ref, dec_ref, bias_ref, sems) = refs[: 2 * NX], refs[2 * NX :]
    copies = fetch([(bias_hbm, bias_ref), (dec_hbm, dec_ref), (enc_hbm, enc_ref)], sems)
    x, core, me = place_ref[0], place_ref[1], place_ref[3]
    number = ids_ref[...] - me * LAT
    ours = ((number >= 0) & (number < LAT)).astype(f32)
    count = dot(ours.astype(bf16), prefix())
    high, low = (number >> 7).astype(f32), (number & 127).astype(f32)
    n = DEVICES // NB
    before = jnp.zeros((n, 1), f32)
    highs = [jnp.zeros((n, ENTRIES), f32) for _ in range(SLOTS)]
    lows = [jnp.zeros((n, ENTRIES), f32) for _ in range(SLOTS)]
    for b in range(NB):
        part = slice(b * n, (b + 1) * n)
        rank = jnp.where(ours[part] > 0.5, count[part] + before, 0.0)
        before = before + count[part][:, ENTRIES - 1 :]
        for k in range(SLOTS):
            mine = rank == k + 1
            highs[k] = highs[k] + jnp.where(mine, high[part], 0.0)
            lows[k] = lows[k] + jnp.where(mine, low[part], 0.0)
    lane = iota((n, ENTRIES), 1)
    table = jnp.zeros((n, ENTRIES), f32)
    for k in range(SLOTS):
        table = table + jnp.where(lane == k, jnp.sum(highs[k], axis=1, keepdims=True), 0.0)
        table = table + jnp.where(lane == SLOTS + k, jnp.sum(lows[k], axis=1, keepdims=True), 0.0)
    pair = iota((PAIRS, n), 0)
    home_x = (x + NX - pair // CHUNK) % NX
    home_core = (core + pair // (CHUNK // 2)) % 2
    group = ((pair // SLOTS) % NZ) * 8 + home_x * 2 + home_core
    found = dot((iota((PAIRS, n), 1) == group).astype(bf16), table.astype(bf16))
    lane = iota((PAIRS, ENTRIES), 1)
    slot = iota((PAIRS, ENTRIES), 0) % SLOTS
    weight = jnp.where(lane == slot, 128.0, jnp.where(lane == SLOTS + slot, 1.0, 0.0))
    number = jnp.sum(found * weight, axis=1, keepdims=True)
    sel = (number == iota((PAIRS, LAT), 1).astype(f32)).astype(f32)
    copies[0].wait()
    bias = jnp.sum(sel * bias_ref[...].astype(f32).reshape(1, LAT), axis=1, keepdims=True)
    bias = jnp.broadcast_to(bias, (PAIRS, IDS)).astype(bf16)
    sel = sel.astype(bf16)
    sel_ref[...] = sel
    copies[1].wait()
    dec = dot(sel, dec_ref[...]).astype(bf16)
    copies[2].wait()
    enc = dot(sel, enc_ref[...], ((1,), (1,))).astype(bf16)
    for i, out in enumerate(outs):
        part = slice(i * PIECE, (i + 1) * PIECE)
        out[:, :D] = dec[part]
        out[:, D : 2 * D] = enc[part]
        out[:, 2 * D :] = bias[part]


def route_kernel(place_ref, ids_ref, onehot_ref):
    x, core, me = place_ref[0], place_ref[1], place_ref[3]
    n = NX * 2 * SLOTS
    row = iota((n, ENTRIES), 0)
    first = me - x * 2 - core + ((x + row // (2 * SLOTS)) % NX) * 2 + (core + row // SLOTS) % 2
    slot = (row % SLOTS + 1).astype(f32)
    ours = []
    for s in range(NCOL):
        number = ids_ref[pl.ds(s * 8 + x * 2 + core, 1), :] - first * LAT
        ours.append(((number >= 0) & (number < LAT)).astype(f32))
    count = dot(jnp.concatenate(ours, axis=0).astype(bf16), prefix())
    chosen = [None] * NCOL
    for z in range(NZ):
        before = jnp.zeros((n, 1), f32)
        for b in range(NB):
            at = b * NZ + z
            here = count[at * n : (at + 1) * n]
            chosen[at] = jnp.where(here + before == slot, ours[at], 0.0)
            before = before + here[:, ENTRIES - 1 :]
    lane = iota((ENTRIES, ENTRIES), 1)
    second = (iota((ENTRIES, ENTRIES), 0) // K == (lane % BLOCK) // 4).astype(bf16)
    spread = dot(jnp.concatenate(chosen, axis=0).astype(bf16), second)
    place = iota((n, ENTRIES), 1) // BLOCK
    per = ENTRIES // BLOCK
    groups = []
    for z in range(NZ):
        tiles = [jnp.zeros((n, ENTRIES), f32) for _ in range(HOME // ENTRIES)]
        for b in range(NB):
            at = b * NZ + z
            part = jnp.where(place == at % per, spread[at * n : (at + 1) * n], 0.0)
            tiles[at // per] = tiles[at // per] + part
        groups.append(jnp.concatenate(tiles, axis=1))
    to, frm = iota((PAIRS, PAIRS), 0), iota((PAIRS, PAIRS), 1)
    source = ((to // SLOTS) % NZ) * n + (to // PIECE) * SLOTS + to % SLOTS
    order = (frm == source).astype(bf16)
    onehot_ref[...] = dot(order, jnp.concatenate(groups, axis=0).astype(bf16)).astype(bf16)


ORDER = ((3, 0), (1, 0), (2, 0), (2, 1), (3, 1), (1, 1), (0, 1), (0, 0))
X_ORDER = (2, 1, 3, 0)


def gathered(refs):
    at = [ORDER.index((i // 2, i % 2)) for i in range(2 * NX)]
    return jnp.concatenate([refs[i][...] for i in at], axis=0)


def in_order(chunks):
    return [chunks[d] for d in X_ORDER]


def collect_kernel(*refs):
    w = gathered(refs[: 2 * NX])
    rows_ref, onehot_ref, sums_ref, code_ref = refs[2 * NX : 2 * NX + 4]
    outs = refs[2 * NX + 4 :]
    onehot = onehot_ref[...]
    home = rows_ref[...]
    code = w[:, 2 * D : 2 * D + 1].astype(f32)
    for q in range(4):
        rows = take_rows(onehot, home, q)
        for d, out in enumerate(outs):
            out[:, q * QUARTER : (q + 1) * QUARTER] = rows[d * CHUNK : (d + 1) * CHUNK]
        enc = w[:, D + q * QUARTER : D + (q + 1) * QUARTER]
        code = code + jnp.sum(rows.astype(f32) * enc.astype(f32), axis=1, keepdims=True)
    code = code.astype(bf16).astype(f32)
    code_ref[...] = jnp.broadcast_to(code, (PAIRS, IDS)).astype(bf16)
    coded = (onehot.astype(f32) * code).astype(bf16)
    lane = iota((1, HOME), 1)
    total = jnp.zeros((HOME, QUARTER), f32)
    for q in range(4):
        pick = jnp.where(lane % 4 == q, coded, jnp.zeros((), bf16))
        total = total + dot(pick, w[:, q * QUARTER : (q + 1) * QUARTER], ((0,), (0,)))
    sums_ref[...] = total.astype(bf16)


def add_parts_kernel(parts_ref, wide_ref, out_ref):
    total = parts_ref[:PART, :].astype(f32)
    for b in range(1, NB):
        total = total + parts_ref[b * PART : (b + 1) * PART, :].astype(f32)
    wide_ref[...] = total
    out_ref[...] = total.astype(bf16)


def residual_kernel(place_ref, wide_ref, p1, p2, p3, home_ref, out_ref, sums_ref):
    rebuilt = wide_ref[...] + (p1[...].astype(f32) + p2[...].astype(f32) + p3[...].astype(f32))
    first = pl.multiple_of(place_ref[2] * PART, PART)
    residual = rebuilt - home_ref[pl.ds(first, PART), :].astype(f32)
    grad = residual.astype(bf16)
    for b in range(NB):
        out_ref[b * PART : (b + 1) * PART, :] = grad
    columns = jnp.sum(residual.reshape(NZ, BLOCK, QUARTER), axis=0) * (1.0 / NZ)
    for q in range(4):
        sums_ref[:, q * QUARTER : (q + 1) * QUARTER] = columns[q : q + 1] + columns[q + 4 : q + 5]
    square = jnp.sum(residual * residual) * (1.0 / (NZ * ROWS * D))
    sums_ref[:, D:] = jnp.full((1, VCOLS), square, f32)


def pre_kernel(onehot_ref, grad_ref, sums_ref, *refs):
    w = gathered(refs[: 2 * NX])
    pre_ref, vec_ref = refs[2 * NX :]
    onehot = onehot_ref[...]
    grad = grad_ref[...]
    pre = jnp.zeros((PAIRS, 1), f32)
    for q in range(4):
        rows = take_rows(onehot, grad, q)
        dec = w[:, q * QUARTER : (q + 1) * QUARTER]
        pre = pre + jnp.sum(rows.astype(f32) * dec.astype(f32), axis=1, keepdims=True)
    pre = jnp.broadcast_to(pre, (PAIRS, IDS)).astype(bf16)
    pre_ref[...] = pre
    term = dot(pre, w[:, D : 2 * D], ((0,), (0,)))
    vec = sums_ref[:, :D] - term[0:1]
    for i in range(VROWS - 1):
        vec_ref[i : i + 1, :] = vec[:, i * VCOLS : (i + 1) * VCOLS]
    vec_ref[VROWS - 1 :, :] = sums_ref[:, D:]


def dispatch_kernel(onehot_ref, grad_ref, code_ref, pre_ref, g0, g1, g2, g3):
    onehot = onehot_ref[...]
    grad = grad_ref[...]
    for q in range(4):
        rows = take_rows(onehot, grad, q)
        for d, out in enumerate((g0, g1, g2, g3)):
            out[:, q * QUARTER : (q + 1) * QUARTER] = rows[d * CHUNK : (d + 1) * CHUNK]
    scalars = jnp.where(iota((PAIRS, IDS), 1) == 0, code_ref[...], pre_ref[...])
    for d, out in enumerate((g0, g1, g2, g3)):
        out[:, D:] = scalars[d * CHUNK : (d + 1) * CHUNK]


def grads_kernel(*refs):
    xs, xs_hbm, dec_hbm = refs[:NX], refs[NX], refs[NX + 1]
    gs, gs_ref, sel_ref = refs[NX + 2 : 2 * NX + 2], refs[2 * NX + 2], refs[2 * NX + 3]
    genc_ref, gdec_ref, bias_ref, x_ref, dec_ref, sems = refs[2 * NX + 4 :]
    pairs = [(dec_hbm, dec_ref)]
    parts = []
    for d in range(NX):
        x, g = xs[X_ORDER.index(d)], gs[X_ORDER.index(d)]
        mine, theirs = pl.ds(d * CHUNK, PIECE), pl.ds(d * CHUNK + PIECE, PIECE)
        here = pl.ds(d * PIECE, PIECE)
        pairs.append((x.at[pl.ds(0, PIECE)], x_ref.at[mine]))
        pairs.append((xs_hbm.at[here], x_ref.at[theirs]))
        parts += [g[:PIECE, :], gs_ref[here, :]]
    copies = fetch(pairs, sems)
    g = jnp.concatenate(parts, axis=0)
    sel = sel_ref[...].astype(f32)
    pre = sel * g[:, D + 1 : D + 2].astype(f32)
    bias_ref[...] = jnp.sum(pre, axis=0)
    codes = (sel * g[:, D : D + 1].astype(f32)).astype(bf16)
    raw = dot(codes, g[:, :D], ((0,), (0,)))
    copies[0].wait()
    dec = dec_ref[...].astype(f32)
    along = jnp.sum(raw * dec, axis=1, keepdims=True)
    norm = jnp.sum(dec * dec, axis=1, keepdims=True)
    gdec_ref[...] = (raw - (along / (norm + 1e-06)) * dec).astype(bf16)
    for c in copies[1:]:
        c.wait()
    genc_ref[...] = dot(x_ref[...], pre.astype(bf16), ((0,), (0,))).astype(bf16)


def vector_kernel(copies, parts_ref, out_ref):
    total = parts_ref[:VROWS, :]
    for i in range(1, parts_ref.shape[0] // VROWS):
        total = total + parts_ref[i * VROWS : (i + 1) * VROWS, :]
    for i in range(copies):
        out_ref[i * VROWS : (i + 1) * VROWS, :] = total


def last_vector_kernel(parts_ref, loss_ref, out_ref):
    total = parts_ref[:VROWS, :]
    for i in range(1, parts_ref.shape[0] // VROWS):
        total = total + parts_ref[i * VROWS : (i + 1) * VROWS, :]
    for i in range(VROWS - 1):
        out_ref[pl.ds(i * VCOLS, VCOLS)] = total[i : i + 1, :].reshape(VCOLS)
    loss_ref[...] = total[VROWS - 1 :, :1]


def pair_vector_kernel(copies, own_ref, other_ref, out_ref):
    total = own_ref[...] + other_ref[...]
    for i in range(copies):
        out_ref[i * VROWS : (i + 1) * VROWS, :] = total


SMEM, VMEM, HBM = pltpu.SMEM, pltpu.VMEM, pltpu.HBM


def call(kernel, name, outs, args, spaces=None, scratch=(), mib=8, flops=None):
    spaces = spaces or [VMEM] * len(args)
    args = [
        pltpu.with_memory_space_constraint(a, HBM) if s is HBM else a for a, s in zip(args, spaces)
    ]
    return pl.pallas_call(
        kernel,
        out_shape=[HBM(o[0], o[1]) if len(o) > 2 else jax.ShapeDtypeStruct(*o) for o in outs],
        in_specs=[pl.BlockSpec(memory_space=s) for s in spaces],
        out_specs=[pl.BlockSpec(memory_space=VMEM) for _ in outs],
        scratch_shapes=list(scratch),
        compiler_params=pltpu.CompilerParams(vmem_limit_bytes=mib * 1024 * 1024),
        name=name,
        cost_estimate=flops and pl.CostEstimate(flops=flops, bytes_accessed=0, transcendentals=0),
    )(*args)


def exchange(x, axes, peers):
    shape = x.shape
    x = x.reshape(peers, shape[0] // peers, shape[1])
    return lax.all_to_all(x, axes, split_axis=0, concat_axis=0).reshape(shape)


def step(x, axis, size, by):
    return lax.ppermute(x, axis, [(i, (i + by) % size) for i in range(size)])


def swap_cores(x):
    return step(x, "core", 2, 1)


def hop(chunks, way):
    out = list(chunks)
    for d in (2, 1, 3):
        out[d] = step(chunks[d], "x", NX, way * d)
    return out


def swap_halves(chunks):
    return swap_cores(jnp.concatenate([c[PIECE:] for c in chunks]))


def to_homes(pieces):
    out = []
    for by_x, by_core in ORDER:
        way = [(x * 2 + c, (x - by_x) % NX * 2 + (c + by_core) % 2) for x in range(NX) for c in range(2)]
        piece = pieces[by_x * 2 + by_core]
        out.append(lax.ppermute(piece, ("x", "core"), way) if by_x or by_core else piece)
    return out


def local(activations, indices, enc_weight, dec_weight, enc_bias, dec_bias):
    index = [lax.axis_index(a).astype(jnp.int32) for a in AXES]
    batch = index[0] * 2 + index[1]
    me = (batch * NZ + index[2]) * 8 + index[3] * 2 + index[4]
    place = jnp.stack([index[3], index[4], batch, me])
    sems = pltpu.SemaphoreType.DMA
    enc_space, dec_space = VMEM((D, LAT), bf16), VMEM((LAT, D), bf16)
    home, ids = call(
        setup_kernel,
        "setup",
        [((HOME, QUARTER), bf16), ((DEVICES, ENTRIES), jnp.int32)],
        [activations, dec_bias, indices],
        [HBM] * 3,
        [VMEM((2, D), bf16), VMEM((D,), f32), VMEM((2, K), jnp.int32), sems((3,))],
    )
    ids = exchange(ids, AXES, DEVICES)
    *ws, sel = call(
        owner_kernel,
        "owner",
        [((PIECE, 2 * D + IDS), bf16)] * (2 * NX) + [((PAIRS, LAT), bf16)],
        [place, ids, enc_weight, dec_weight, enc_bias],
        [SMEM, VMEM, HBM, HBM, HBM],
        [enc_space, dec_space, VMEM((LAT,), bf16), sems((3,))],
        mib=20,
    )
    (onehot,) = call(route_kernel, "route", [((PAIRS, HOME), bf16)], [place, ids], [SMEM, VMEM], flops=10**11)
    home, _ = lax.optimization_barrier((home, sel))
    home = exchange(home, AXES[:3], NCOL)
    ws = to_homes(ws)
    parts, code, *xs = call(
        collect_kernel,
        "collect",
        [((HOME, QUARTER), bf16), ((PAIRS, IDS), bf16)] + [((CHUNK, D), bf16, HBM)] * NX,
        [*ws, home, onehot],
        mib=12,
    )
    xs = hop(xs, 1)
    parts = exchange(parts, BATCH, NB)
    wide, part = call(
        add_parts_kernel, "add_parts", [((PART, QUARTER), f32), ((PART, QUARTER), bf16)], [parts]
    )
    others = [step(part, "z_hi", NZ, d) for d in range(1, NZ)]
    others, xs = lax.optimization_barrier((others, xs))
    grad, sums = call(
        residual_kernel,
        "residual",
        [((HOME, QUARTER), bf16), ((1, D + VCOLS), f32)],
        [place, wide] + others + [home],
        [SMEM] + [VMEM] * 5,
    )
    grad = exchange(grad, BATCH, NB)
    pre, vec = call(
        pre_kernel,
        "pre",
        [((PAIRS, IDS), bf16), ((VROWS, VCOLS), f32)],
        [onehot, grad, sums, *ws],
        mib=12,
    )
    gs = call(
        dispatch_kernel,
        "dispatch",
        [((CHUNK, WIDE), bf16)] * NX,
        [onehot, grad, code, pre],
    )
    gs = hop(gs, 1)

    def spread(kernel, name, copies, *args):
        bound = lambda *refs: kernel(copies, *refs)
        return call(bound, name, [((copies * VROWS, VCOLS), f32)], args)[0]

    vec = spread(pair_vector_kernel, "vector_cores", 8, vec, swap_cores(vec))
    vec, gs = lax.optimization_barrier((exchange(vec, ("z_lo", "z_hi"), 8), gs))
    grad_enc, grad_dec, grad_encbias = call(
        grads_kernel,
        "grads",
        [((D, LAT), bf16), ((LAT, D), bf16), ((LAT,), f32)],
        [*in_order(xs), swap_halves(xs), dec_weight, *in_order(gs), swap_halves(gs), sel],
        [HBM] * (NX + 2) + [VMEM] * (NX + 2),
        [VMEM((PAIRS, D), bf16), dec_space, sems((2 * NX + 1,))],
        mib=32,
    )
    vec = spread(vector_kernel, "vector_z", 16, vec)
    vec = exchange(vec, ("y", "x"), 16)
    vec, grad_enc, grad_dec = lax.optimization_barrier((vec, grad_enc, grad_dec))
    loss, grad_decbias = call(
        last_vector_kernel,
        "vector_yx",
        [((1, 1), f32), ((D,), f32)],
        [vec],
    )
    return loss.reshape(()), grad_enc, grad_dec, grad_encbias, grad_decbias


def solution(mesh):
    split = Mesh(mesh.devices.reshape(SIZES), AXES)
    return jax.shard_map(
        local,
        mesh=split,
        in_specs=(P(AXES, None), P(AXES, None), P(None, AXES), P(AXES, None), P(AXES), P()),
        out_specs=(P(), P(None, AXES), P(AXES, None), P(AXES), P()),
        check_vma=False,
    )
```

```python
import jax
import jax.numpy as jnp
from jax import lax
from jax.experimental import pallas as pl
from jax.experimental.pallas import tpu as pltpu
from jax.sharding import Mesh, PartitionSpec as P

bf16 = jnp.bfloat16
f32 = jnp.float32

AXES = ("y", "z_lo", "z_hi", "x", "core")
SIZES = (4, 2, 4, 4, 2)
BATCH = ("y", "z_lo")

D = 3584
QUARTER = D // 4
LAT = 384
NB = 8
NZ = 4
NX = 4
NCOL = NB * NZ
SLOTS = 4
K = 64
ENTRIES = 2 * K
IDS = 128
WIDE = D + IDS
PAIRS = 128
CHUNK = PAIRS // NX
PIECE = CHUNK // 2
BLOCK = 8
HOME = NCOL * BLOCK
PART = NZ * BLOCK
ROWS = 512
DEVICES = 256
VROWS, VCOLS = 8, 512


def dot(a, b, dims=((1,), (0,))):
    return lax.dot_general(a, b, (dims, ((), ())), preferred_element_type=f32)


def iota(shape, axis):
    return lax.broadcasted_iota(jnp.int32, shape, axis)


def quarters(row):
    return [row[:, q * QUARTER : (q + 1) * QUARTER] for q in range(4)]


def fetch(pairs, sems):
    copies = [pltpu.make_async_copy(a, b, sems.at[i]) for i, (a, b) in enumerate(pairs)]
    for c in copies:
        c.start()
    return copies


def numbers_kernel(idx_hbm, ids_ref, idx_ref, sems):
    for c in fetch([(idx_hbm, idx_ref)], sems):
        c.wait()
    idx = jnp.concatenate([idx_ref[0:1, :], idx_ref[1:2, :]], axis=1)
    ids_ref[...] = jnp.broadcast_to(idx, ids_ref.shape)


def setup_kernel(act_hbm, bias_hbm, out_ref, act_ref, bias_ref, sems):
    for c in fetch([(act_hbm, act_ref), (bias_hbm, bias_ref)], sems):
        c.wait()
    centred = act_ref[...].astype(f32) - bias_ref[...].reshape(1, D)
    rows = jnp.concatenate(quarters(centred[0:1]) + quarters(centred[1:2]), axis=0)
    block = jnp.concatenate([rows, rows], axis=0).astype(bf16)
    for i in range(out_ref.shape[0] // (2 * BLOCK)):
        out_ref[i * 2 * BLOCK : (i + 1) * 2 * BLOCK, :] = block


def take_rows(onehot, rows, q):
    lane = iota((1, HOME), 1)
    return dot(jnp.where(lane % 4 == q, onehot, jnp.zeros((), bf16)), rows).astype(bf16)


def prefix():
    return (iota((ENTRIES, ENTRIES), 0) <= iota((ENTRIES, ENTRIES), 1)).astype(bf16)


def owner_kernel(place_ref, ids_ref, enc_hbm, dec_hbm, bias_hbm, *refs):
    outs, (sel_ref, enc_ref, dec_ref, bias_ref, sems) = refs[: 2 * NX], refs[2 * NX :]
    copies = fetch([(bias_hbm, bias_ref), (dec_hbm, dec_ref), (enc_hbm, enc_ref)], sems)
    x, core, me = place_ref[0], place_ref[1], place_ref[3]
    number = ids_ref[...] - me * LAT
    ours = ((number >= 0) & (number < LAT)).astype(f32)
    count = dot(ours.astype(bf16), prefix())
    high, low = (number >> 7).astype(f32), (number & 127).astype(f32)
    n = DEVICES // NB
    before = jnp.zeros((n, 1), f32)
    highs = [jnp.zeros((n, ENTRIES), f32) for _ in range(SLOTS)]
    lows = [jnp.zeros((n, ENTRIES), f32) for _ in range(SLOTS)]
    for b in range(NB):
        part = slice(b * n, (b + 1) * n)
        rank = jnp.where(ours[part] > 0.5, count[part] + before, 0.0)
        before = before + count[part][:, ENTRIES - 1 :]
        for k in range(SLOTS):
            mine = rank == k + 1
            highs[k] = highs[k] + jnp.where(mine, high[part], 0.0)
            lows[k] = lows[k] + jnp.where(mine, low[part], 0.0)
    lane = iota((n, ENTRIES), 1)
    table = jnp.zeros((n, ENTRIES), f32)
    for k in range(SLOTS):
        table = table + jnp.where(lane == k, jnp.sum(highs[k], axis=1, keepdims=True), 0.0)
        table = table + jnp.where(lane == SLOTS + k, jnp.sum(lows[k], axis=1, keepdims=True), 0.0)
    pair = iota((PAIRS, n), 0)
    home_x = (x + NX - pair // CHUNK) % NX
    home_core = (core + pair // (CHUNK // 2)) % 2
    group = ((pair // SLOTS) % NZ) * 8 + home_x * 2 + home_core
    found = dot((iota((PAIRS, n), 1) == group).astype(bf16), table.astype(bf16))
    lane = iota((PAIRS, ENTRIES), 1)
    slot = iota((PAIRS, ENTRIES), 0) % SLOTS
    weight = jnp.where(lane == slot, 128.0, jnp.where(lane == SLOTS + slot, 1.0, 0.0))
    number = jnp.sum(found * weight, axis=1, keepdims=True)
    sel = (number == iota((PAIRS, LAT), 1).astype(f32)).astype(f32)
    copies[0].wait()
    bias = jnp.sum(sel * bias_ref[...].astype(f32).reshape(1, LAT), axis=1, keepdims=True)
    bias = jnp.broadcast_to(bias, (PAIRS, IDS)).astype(bf16)
    sel = sel.astype(bf16)
    sel_ref[...] = sel
    copies[1].wait()
    dec = dot(sel, dec_ref[...]).astype(bf16)
    copies[2].wait()
    enc = dot(sel, enc_ref[...], ((1,), (1,))).astype(bf16)
    for i, out in enumerate(outs):
        part = slice(i * PIECE, (i + 1) * PIECE)
        out[:, :D] = dec[part]
        out[:, D : 2 * D] = enc[part]
        out[:, 2 * D :] = bias[part]


def route_kernel(place_ref, ids_ref, onehot_ref):
    x, core, me = place_ref[0], place_ref[1], place_ref[3]
    n = NX * 2 * SLOTS
    row = iota((n, ENTRIES), 0)
    first = me - x * 2 - core + ((x + row // (2 * SLOTS)) % NX) * 2 + (core + row // SLOTS) % 2
    slot = (row % SLOTS + 1).astype(f32)
    ours = []
    for s in range(NCOL):
        number = ids_ref[pl.ds(s * 8 + x * 2 + core, 1), :] - first * LAT
        ours.append(((number >= 0) & (number < LAT)).astype(f32))
    count = dot(jnp.concatenate(ours, axis=0).astype(bf16), prefix())
    chosen = [None] * NCOL
    for z in range(NZ):
        before = jnp.zeros((n, 1), f32)
        for b in range(NB):
            at = b * NZ + z
            here = count[at * n : (at + 1) * n]
            chosen[at] = jnp.where(here + before == slot, ours[at], 0.0)
            before = before + here[:, ENTRIES - 1 :]
    lane = iota((ENTRIES, ENTRIES), 1)
    second = (iota((ENTRIES, ENTRIES), 0) // K == (lane % BLOCK) // 4).astype(bf16)
    spread = dot(jnp.concatenate(chosen, axis=0).astype(bf16), second)
    place = iota((n, ENTRIES), 1) // BLOCK
    per = ENTRIES // BLOCK
    groups = []
    for z in range(NZ):
        tiles = [jnp.zeros((n, ENTRIES), f32) for _ in range(HOME // ENTRIES)]
        for b in range(NB):
            at = b * NZ + z
            part = jnp.where(place == at % per, spread[at * n : (at + 1) * n], 0.0)
            tiles[at // per] = tiles[at // per] + part
        groups.append(jnp.concatenate(tiles, axis=1))
    to, frm = iota((PAIRS, PAIRS), 0), iota((PAIRS, PAIRS), 1)
    source = ((to // SLOTS) % NZ) * n + (to // PIECE) * SLOTS + to % SLOTS
    order = (frm == source).astype(bf16)
    onehot_ref[...] = dot(order, jnp.concatenate(groups, axis=0).astype(bf16)).astype(bf16)


ORDER = ((3, 0), (1, 0), (2, 0), (2, 1), (3, 1), (1, 1), (0, 1), (0, 0))
X_ORDER = (2, 1, 3, 0)


def gathered(refs):
    at = [ORDER.index((i // 2, i % 2)) for i in range(2 * NX)]
    return jnp.concatenate([refs[i][...] for i in at], axis=0)


def in_order(chunks):
    return [chunks[d] for d in X_ORDER]


def collect_kernel(*refs):
    w = gathered(refs[: 2 * NX])
    rows_ref, onehot_ref, sums_ref, code_ref = refs[2 * NX : 2 * NX + 4]
    outs = refs[2 * NX + 4 :]
    onehot = onehot_ref[...]
    home = rows_ref[...]
    code = w[:, 2 * D : 2 * D + 1].astype(f32)
    for q in range(4):
        rows = take_rows(onehot, home, q)
        for d, out in enumerate(outs):
            out[:, q * QUARTER : (q + 1) * QUARTER] = rows[d * CHUNK : (d + 1) * CHUNK]
        enc = w[:, D + q * QUARTER : D + (q + 1) * QUARTER]
        code = code + jnp.sum(rows.astype(f32) * enc.astype(f32), axis=1, keepdims=True)
    code = code.astype(bf16).astype(f32)
    code_ref[...] = jnp.broadcast_to(code, (PAIRS, IDS)).astype(bf16)
    coded = (onehot.astype(f32) * code).astype(bf16)
    lane = iota((1, HOME), 1)
    total = jnp.zeros((HOME, QUARTER), f32)
    for q in range(4):
        pick = jnp.where(lane % 4 == q, coded, jnp.zeros((), bf16))
        total = total + dot(pick, w[:, q * QUARTER : (q + 1) * QUARTER], ((0,), (0,)))
    sums_ref[...] = total.astype(bf16)


def add_parts_kernel(parts_ref, wide_ref, out_ref):
    total = parts_ref[:PART, :].astype(f32)
    for b in range(1, NB):
        total = total + parts_ref[b * PART : (b + 1) * PART, :].astype(f32)
    wide_ref[...] = total
    out_ref[...] = total.astype(bf16)


def residual_kernel(place_ref, wide_ref, p1, p2, p3, home_ref, out_ref, sums_ref):
    rebuilt = wide_ref[...] + (p1[...].astype(f32) + p2[...].astype(f32) + p3[...].astype(f32))
    first = pl.multiple_of(place_ref[2] * PART, PART)
    residual = rebuilt - home_ref[pl.ds(first, PART), :].astype(f32)
    grad = residual.astype(bf16)
    for b in range(NB):
        out_ref[b * PART : (b + 1) * PART, :] = grad
    columns = jnp.sum(residual.reshape(NZ, BLOCK, QUARTER), axis=0) * (1.0 / NZ)
    for q in range(4):
        sums_ref[:, q * QUARTER : (q + 1) * QUARTER] = columns[q : q + 1] + columns[q + 4 : q + 5]
    square = jnp.sum(residual * residual) * (1.0 / (NZ * ROWS * D))
    sums_ref[:, D:] = jnp.full((1, VCOLS), square, f32)


def pre_kernel(onehot_ref, grad_ref, sums_ref, *refs):
    w = gathered(refs[: 2 * NX])
    pre_ref, vec_ref = refs[2 * NX :]
    onehot = onehot_ref[...]
    grad = grad_ref[...]
    pre = jnp.zeros((PAIRS, 1), f32)
    for q in range(4):
        rows = take_rows(onehot, grad, q)
        dec = w[:, q * QUARTER : (q + 1) * QUARTER]
        pre = pre + jnp.sum(rows.astype(f32) * dec.astype(f32), axis=1, keepdims=True)
    pre = jnp.broadcast_to(pre, (PAIRS, IDS)).astype(bf16)
    pre_ref[...] = pre
    term = dot(pre, w[:, D : 2 * D], ((0,), (0,)))
    vec = sums_ref[:, :D] - term[0:1]
    for i in range(VROWS - 1):
        vec_ref[i : i + 1, :] = vec[:, i * VCOLS : (i + 1) * VCOLS]
    vec_ref[VROWS - 1 :, :] = sums_ref[:, D:]


def dispatch_kernel(onehot_ref, grad_ref, code_ref, pre_ref, g0, g1, g2, g3):
    onehot = onehot_ref[...]
    grad = grad_ref[...]
    for q in range(4):
        rows = take_rows(onehot, grad, q)
        for d, out in enumerate((g0, g1, g2, g3)):
            out[:, q * QUARTER : (q + 1) * QUARTER] = rows[d * CHUNK : (d + 1) * CHUNK]
    scalars = jnp.where(iota((PAIRS, IDS), 1) == 0, code_ref[...], pre_ref[...])
    for d, out in enumerate((g0, g1, g2, g3)):
        out[:, D:] = scalars[d * CHUNK : (d + 1) * CHUNK]


def grads_kernel(*refs):
    xs, xs_hbm, dec_hbm = refs[:NX], refs[NX], refs[NX + 1]
    gs, gs_ref, sel_ref = refs[NX + 2 : 2 * NX + 2], refs[2 * NX + 2], refs[2 * NX + 3]
    genc_ref, gdec_ref, bias_ref, x_ref, dec_ref, sems = refs[2 * NX + 4 :]
    pairs = [(dec_hbm, dec_ref)]
    parts = []
    for d in range(NX):
        x, g = xs[X_ORDER.index(d)], gs[X_ORDER.index(d)]
        mine, theirs = pl.ds(d * CHUNK, PIECE), pl.ds(d * CHUNK + PIECE, PIECE)
        here = pl.ds(d * PIECE, PIECE)
        pairs.append((x.at[pl.ds(0, PIECE)], x_ref.at[mine]))
        pairs.append((xs_hbm.at[here], x_ref.at[theirs]))
        parts += [g[:PIECE, :], gs_ref[here, :]]
    copies = fetch(pairs, sems)
    g = jnp.concatenate(parts, axis=0)
    sel = sel_ref[...].astype(f32)
    pre = sel * g[:, D + 1 : D + 2].astype(f32)
    bias_ref[...] = jnp.sum(pre, axis=0)
    codes = (sel * g[:, D : D + 1].astype(f32)).astype(bf16)
    raw = dot(codes, g[:, :D], ((0,), (0,)))
    copies[0].wait()
    dec = dec_ref[...].astype(f32)
    along = jnp.sum(raw * dec, axis=1, keepdims=True)
    norm = jnp.sum(dec * dec, axis=1, keepdims=True)
    gdec_ref[...] = (raw - (along / (norm + 1e-06)) * dec).astype(bf16)
    for c in copies[1:]:
        c.wait()
    genc_ref[...] = dot(x_ref[...], pre.astype(bf16), ((0,), (0,))).astype(bf16)


def vector_kernel(copies, parts_ref, out_ref):
    total = parts_ref[:VROWS, :]
    for i in range(1, parts_ref.shape[0] // VROWS):
        total = total + parts_ref[i * VROWS : (i + 1) * VROWS, :]
    for i in range(copies):
        out_ref[i * VROWS : (i + 1) * VROWS, :] = total


def last_vector_kernel(parts_ref, loss_ref, out_ref):
    total = parts_ref[:VROWS, :]
    for i in range(1, parts_ref.shape[0] // VROWS):
        total = total + parts_ref[i * VROWS : (i + 1) * VROWS, :]
    for i in range(VROWS - 1):
        out_ref[pl.ds(i * VCOLS, VCOLS)] = total[i : i + 1, :].reshape(VCOLS)
    loss_ref[...] = total[VROWS - 1 :, :1]


def pair_vector_kernel(copies, own_ref, other_ref, out_ref):
    total = own_ref[...] + other_ref[...]
    for i in range(copies):
        out_ref[i * VROWS : (i + 1) * VROWS, :] = total


SMEM, VMEM, HBM = pltpu.SMEM, pltpu.VMEM, pltpu.HBM


def call(kernel, name, outs, args, spaces=None, scratch=(), mib=8, flops=None):
    spaces = spaces or [VMEM] * len(args)
    args = [
        pltpu.with_memory_space_constraint(a, HBM) if s is HBM else a for a, s in zip(args, spaces)
    ]
    return pl.pallas_call(
        kernel,
        out_shape=[HBM(o[0], o[1]) if len(o) > 2 else jax.ShapeDtypeStruct(*o) for o in outs],
        in_specs=[pl.BlockSpec(memory_space=s) for s in spaces],
        out_specs=[pl.BlockSpec(memory_space=VMEM) for _ in outs],
        scratch_shapes=list(scratch),
        compiler_params=pltpu.CompilerParams(vmem_limit_bytes=mib * 1024 * 1024),
        name=name,
        cost_estimate=flops and pl.CostEstimate(flops=flops, bytes_accessed=0, transcendentals=0),
    )(*args)


def exchange(x, axes, peers):
    shape = x.shape
    x = x.reshape(peers, shape[0] // peers, shape[1])
    return lax.all_to_all(x, axes, split_axis=0, concat_axis=0).reshape(shape)


def step(x, axis, size, by):
    return lax.ppermute(x, axis, [(i, (i + by) % size) for i in range(size)])


def swap_cores(x):
    return step(x, "core", 2, 1)


def hop(chunks, way):
    out = list(chunks)
    for d in (2, 1, 3):
        out[d] = step(chunks[d], "x", NX, way * d)
    return out


def swap_halves(chunks):
    return swap_cores(jnp.concatenate([c[PIECE:] for c in chunks]))


def to_homes(pieces):
    out = []
    for by_x, by_core in ORDER:
        way = [(x * 2 + c, (x - by_x) % NX * 2 + (c + by_core) % 2) for x in range(NX) for c in range(2)]
        piece = pieces[by_x * 2 + by_core]
        out.append(lax.ppermute(piece, ("x", "core"), way) if by_x or by_core else piece)
    return out


def local(activations, indices, enc_weight, dec_weight, enc_bias, dec_bias):
    index = [lax.axis_index(a).astype(jnp.int32) for a in AXES]
    batch = index[0] * 2 + index[1]
    me = (batch * NZ + index[2]) * 8 + index[3] * 2 + index[4]
    place = jnp.stack([index[3], index[4], batch, me])
    sems = pltpu.SemaphoreType.DMA
    enc_space, dec_space = VMEM((D, LAT), bf16), VMEM((LAT, D), bf16)
    (ids,) = call(
        numbers_kernel,
        "numbers",
        [((DEVICES, ENTRIES), jnp.int32)],
        [indices],
        [HBM],
        [VMEM((2, K), jnp.int32), sems((1,))],
    )
    (home,) = call(
        setup_kernel,
        "setup",
        [((HOME, QUARTER), bf16)],
        [activations, dec_bias],
        [HBM] * 2,
        [VMEM((2, D), bf16), VMEM((D,), f32), sems((2,))],
    )
    ids = exchange(ids, AXES, DEVICES)
    *ws, sel = call(
        owner_kernel,
        "owner",
        [((PIECE, 2 * D + IDS), bf16)] * (2 * NX) + [((PAIRS, LAT), bf16)],
        [place, ids, enc_weight, dec_weight, enc_bias],
        [SMEM, VMEM, HBM, HBM, HBM],
        [enc_space, dec_space, VMEM((LAT,), bf16), sems((3,))],
        mib=20,
    )
    (onehot,) = call(route_kernel, "route", [((PAIRS, HOME), bf16)], [place, ids], [SMEM, VMEM], flops=10**11)
    home, _ = lax.optimization_barrier((home, sel))
    home = exchange(home, AXES[:3], NCOL)
    ws = to_homes(ws)
    parts, code, *xs = call(
        collect_kernel,
        "collect",
        [((HOME, QUARTER), bf16), ((PAIRS, IDS), bf16)] + [((CHUNK, D), bf16, HBM)] * NX,
        [*ws, home, onehot],
        mib=12,
    )
    xs = hop(xs, 1)
    parts = exchange(parts, BATCH, NB)
    wide, part = call(
        add_parts_kernel, "add_parts", [((PART, QUARTER), f32), ((PART, QUARTER), bf16)], [parts]
    )
    others = [step(part, "z_hi", NZ, d) for d in range(1, NZ)]
    others, xs = lax.optimization_barrier((others, xs))
    grad, sums = call(
        residual_kernel,
        "residual",
        [((HOME, QUARTER), bf16), ((1, D + VCOLS), f32)],
        [place, wide] + others + [home],
        [SMEM] + [VMEM] * 5,
    )
    grad = exchange(grad, BATCH, NB)
    pre, vec = call(
        pre_kernel,
        "pre",
        [((PAIRS, IDS), bf16), ((VROWS, VCOLS), f32)],
        [onehot, grad, sums, *ws],
        mib=12,
    )
    gs = call(
        dispatch_kernel,
        "dispatch",
        [((CHUNK, WIDE), bf16)] * NX,
        [onehot, grad, code, pre],
    )
    gs = hop(gs, 1)

    def spread(kernel, name, copies, *args):
        bound = lambda *refs: kernel(copies, *refs)
        return call(bound, name, [((copies * VROWS, VCOLS), f32)], args)[0]

    vec, swapped = lax.optimization_barrier((vec, swap_halves(xs)))
    vec = spread(pair_vector_kernel, "vector_cores", 8, vec, swap_cores(vec))
    vec, gs = lax.optimization_barrier((exchange(vec, ("z_lo", "z_hi"), 8), gs))
    grad_enc, grad_dec, grad_encbias = call(
        grads_kernel,
        "grads",
        [((D, LAT), bf16), ((LAT, D), bf16), ((LAT,), f32)],
        [*in_order(xs), swapped, dec_weight, *in_order(gs), swap_halves(gs), sel],
        [HBM] * (NX + 2) + [VMEM] * (NX + 2),
        [VMEM((PAIRS, D), bf16), dec_space, sems((2 * NX + 1,))],
        mib=32,
    )
    vec = spread(vector_kernel, "vector_z", 16, vec)
    vec = exchange(vec, ("y", "x"), 16)
    vec, grad_enc, grad_dec = lax.optimization_barrier((vec, grad_enc, grad_dec))
    loss, grad_decbias = call(
        last_vector_kernel,
        "vector_yx",
        [((1, 1), f32), ((D,), f32)],
        [vec],
    )
    return loss.reshape(()), grad_enc, grad_dec, grad_encbias, grad_decbias


def solution(mesh):
    split = Mesh(mesh.devices.reshape(SIZES), AXES)
    return jax.shard_map(
        local,
        mesh=split,
        in_specs=(P(AXES, None), P(AXES, None), P(None, AXES), P(AXES, None), P(AXES), P()),
        out_specs=(P(), P(None, AXES), P(AXES, None), P(AXES), P()),
        check_vma=False,
    )
```
